256 devices in a mesh: gx: 16 (over y, z_lo), gy: 8 (over x, core), ga: 2 (over z_hi).
Axes of the slice: x: 4, y: 4, z: 8 (z_hi: 2, z_lo: 4; z = z_hi * 4 + z_lo), core: 2. Of those that a mesh axis runs over, the one named last changes fastest.
Arguments:
- thermal_anomaly: float32 [20, 1024, 4096], P(None, 'gy', ('gx', 'ga')), may hold values from -6 to 6
- sheared_current: float32 [2, 20, 1024, 4096], P(None, None, 'gy', ('gx', 'ga')), may hold values from -3 to 3
- mixing_coefficient: float32 [20, 1024, 4096], P(None, 'gy', ('gx', 'ga')), may hold values from 0.05 to 2
- surface_elevation: float32 [1024, 4096], P('gy', ('gx', 'ga')), may hold values from -2 to 2
- depth_integrated_current: float32 [2, 1024, 4096], P(None, 'gy', ('gx', 'ga')), may hold values from -3 to 3
- water_column_flag: int32 [1024, 4096], P('gy', ('gx', 'ga')), may hold values from 0 to 1
- wet_layer_counts: int32 [1024, 4096], P('gy', ('gx', 'ga')), may hold values from 1 to 20
Outputs:
- mixed: float32 [20, 1024, 4096], P(None, 'gy', ('gx', 'ga'))
- velocity_out: float32 [2, 20, 1024, 4096], P(None, None, 'gy', ('gx', 'ga'))
- height_out: float32 [1024, 4096], P('gy', ('gx', 'ga'))
- transport_out: float32 [2, 1024, 4096], P(None, 'gy', ('gx', 'ga'))
The draws below stay inside these ranges and needn't reach their ends.
All inputs are finite; a program needn't handle non-finite values.
Results may differ from the reference program's by a relative error of at most 0.00002.
Values sent between devices are 32-bit elements; how exact they have to be, the bound alone decides.
No kernel may reach another device: no remote copies, remote signals or barrier semaphores. Data moves between devices by JAX's collectives and lax.ppermute only.
A program may use at most 64 MiB of HBM per device.

```python
import math
import jax
import jax.numpy as jnp

CX = 128
CY = 128
DEPTH_LAYERS = 20
NSUB = 4
LONGITUDE_COUNT = 4096
LATITUDE_COUNT = 1024


def draw_water_column_flag(key, part):
    key = jax.random.fold_in(key, 11)
    tile_key = jax.random.fold_in(key, 1)
    cell_key = jax.random.fold_in(key, 2)
    shares = jax.random.randint(tile_key, (LATITUDE_COUNT // CY, LONGITUDE_COUNT // CX), 20, 96)
    tiles = jnp.repeat(jnp.repeat(shares, CY, axis=0), CX, axis=1)
    cells = jax.random.randint(cell_key, (LATITUDE_COUNT, LONGITUDE_COUNT), 0, 100)
    return (cells < tiles).astype(jnp.int32)


def set_ends(array, stream_key, smallest, top_value):
    longest = array.shape.index(max(array.shape))
    spots = []
    for shift in (0, 1):
        where = [jax.random.randint(jax.random.fold_in(stream_key, axis), (), 0, length) for axis, length in enumerate(array.shape)]
        where[longest] = (where[longest] + shift) % array.shape[longest]
        spots.append(tuple(where))
    return array.at[spots[0]].set(smallest).at[spots[1]].set(top_value)


def steps_of(key, shape, cuts, least, largest):
    factor_of = 1.0
    for axis_at, shards_of in cuts:
        steps = jax.random.uniform(jax.random.fold_in(jax.random.fold_in(key, 6), axis_at), (shards_of,), jnp.float32, least / len(cuts), largest / len(cuts))
        factor_of = factor_of * jnp.repeat(jnp.exp(steps), shape[axis_at] // shards_of).reshape((-1,) + (1,) * (len(shape) - 1 - axis_at))
    return factor_of


def noise(own_key, dims, scale, limit, cuts=(), kind=jnp.bfloat16):
    drawn = scale * jax.random.normal(own_key, dims, jnp.float32)
    if cuts:
        drawn = drawn * steps_of(own_key, dims, cuts, -0.22, 0.18)
    return jnp.clip(drawn, -limit, limit).astype(kind)


def setup_inputs(seed: int = 0) -> dict:
    splits = jax.random.split(jax.random.key(seed), 8)
    return {
        "thermal_anomaly": noise(splits[0], (DEPTH_LAYERS, LATITUDE_COUNT, LONGITUDE_COUNT), 1.0, 6.0, ((1, 8), (2, 32)), jnp.float32),
        "sheared_current": noise(splits[1], (2, DEPTH_LAYERS, LATITUDE_COUNT, LONGITUDE_COUNT), 0.5, 3.0, ((2, 8), (3, 32)), jnp.float32),
        "mixing_coefficient": jnp.clip(jnp.exp(math.log(2.0) - 3.6888794 * jax.random.uniform(splits[2], (DEPTH_LAYERS, LATITUDE_COUNT, LONGITUDE_COUNT), jnp.float32) ** steps_of(splits[2], (DEPTH_LAYERS, LATITUDE_COUNT, LONGITUDE_COUNT), ((1, 8), (2, 32)), -0.2, 0.2)), 0.05, 2.0),
        "surface_elevation": noise(splits[3], (LATITUDE_COUNT, LONGITUDE_COUNT), 0.3, 2.0, ((0, 8), (1, 32)), jnp.float32),
        "depth_integrated_current": noise(splits[4], (2, LATITUDE_COUNT, LONGITUDE_COUNT), 0.5, 3.0, ((1, 8), (2, 32)), jnp.float32),
        "water_column_flag": draw_water_column_flag(jax.random.fold_in(splits[7], 71), 0),
        "wet_layer_counts": set_ends(jax.random.randint(splits[6], (LATITUDE_COUNT, LONGITUDE_COUNT), 1, DEPTH_LAYERS + 1), jax.random.fold_in(splits[6], 1), 1, DEPTH_LAYERS).astype(jnp.int32),
    }


TRANSPORT_SPEED = 0.2
MIXING = 1.0
THERMAL_EXPANSION = 0.05
TIMESTEP = 0.2
SUBSTEP = 0.3
GRAVITY = 1.0


def mix_column(source, mixing_coefficient, water_indicator):
    depth = source.shape[0]
    coupling = [MIXING * 0.5 * (mixing_coefficient[level] + mixing_coefficient[level + 1]) * water_indicator[level] * water_indicator[level + 1] for level in range(depth - 1)]
    ratios = []
    values = []
    for level in range(depth):
        lower = coupling[level - 1] if level > 0 else 0.0
        upper = coupling[level] if level < depth - 1 else 0.0
        diagonal = 1.0 + lower + upper
        if level == 0:
            divisor = diagonal
            carried = source[0]
        else:
            divisor = diagonal + lower * ratios[-1]
            carried = source[level] + lower * values[-1]
        ratios.append(-upper / divisor)
        values.append(carried / divisor)
    result = [values[-1]]
    for level in range(depth - 2, -1, -1):
        result.append(values[level] - ratios[level] * result[-1])
    return jnp.stack(result[::-1])


def longitude_increment(field):
    return (jnp.roll(field, -1, -1) - jnp.roll(field, 1, -1)) * 0.5


def latitude_increment(field):
    widths = [(0, 0)] * (field.ndim - 2) + [(1, 1), (0, 0)]
    padded = jnp.pad(field, widths)
    return (padded[..., 2:, :] - padded[..., :-2, :]) * 0.5


def reference(thermal_anomaly, sheared_current, mixing_coefficient, surface_elevation, depth_integrated_current, water_column_flag, wet_layer_counts):
    layer_thicknesses = thermal_anomaly.shape[0]
    wetness = water_column_flag.astype(jnp.float32)
    level_ids = jnp.arange(layer_thicknesses, dtype=jnp.int32)[:, None, None]
    water_indicator = wetness[None] * (level_ids < wet_layer_counts[None]).astype(jnp.float32)
    east_current_speed = sheared_current[0]
    north_current_speed = sheared_current[1]
    east_face_transfer = east_current_speed * thermal_anomaly * water_indicator
    north_face_transfer = north_current_speed * thermal_anomaly * water_indicator
    hydrostatic_load = THERMAL_EXPANSION * jnp.cumsum(thermal_anomaly * water_indicator, axis=0)
    carried_scalar = water_indicator * (thermal_anomaly - TRANSPORT_SPEED * (longitude_increment(east_face_transfer) + latitude_increment(north_face_transfer)))
    mixed = mix_column(carried_scalar, mixing_coefficient, water_indicator)
    row_index = jnp.arange(LATITUDE_COUNT, dtype=jnp.int32)
    coriolis = (0.3 + 0.4 * row_index.astype(jnp.float32) / LATITUDE_COUNT)[:, None]
    east_new = water_indicator * (east_current_speed + TIMESTEP * (coriolis * north_current_speed - longitude_increment(hydrostatic_load)))
    north_new = water_indicator * (north_current_speed + TIMESTEP * (-coriolis * east_current_speed - latitude_increment(hydrostatic_load)))
    forcing_east = jnp.sum(water_indicator * (east_new - east_current_speed), axis=0) / layer_thicknesses
    forcing_north = jnp.sum(water_indicator * (north_new - north_current_speed), axis=0) / layer_thicknesses
    depth = wetness * wet_layer_counts.astype(jnp.float32) / layer_thicknesses
    surface = surface_elevation
    east_bar = depth_integrated_current[0]
    north_bar = depth_integrated_current[1]
    for step in range(NSUB):
        east_next = wetness * (east_bar + SUBSTEP * (-GRAVITY * depth * longitude_increment(surface) + forcing_east))
        north_next = wetness * (north_bar + SUBSTEP * (-GRAVITY * depth * latitude_increment(surface) + forcing_north))
        surface = surface - SUBSTEP * wetness * (longitude_increment(east_next) + latitude_increment(north_next))
        east_bar = east_next
        north_bar = north_next
    count = jnp.maximum(jnp.sum(water_indicator, axis=0), 1.0)
    east_out = water_indicator * (east_new - jnp.sum(water_indicator * east_new, axis=0) / count + east_bar)
    north_out = water_indicator * (north_new - jnp.sum(water_indicator * north_new, axis=0) / count + north_bar)
    return mixed, jnp.stack([east_out, north_out]), surface, jnp.stack([east_bar, north_bar])
```

```python
import functools

import jax
import jax.numpy as jnp
from jax import lax
from jax.experimental import pallas as pl
from jax.experimental.pallas import tpu as pltpu
from jax.sharding import PartitionSpec as P

NSUB = 4
W = 8
TRANSPORT_SPEED = 0.2
MIXING = 1.0
THERMAL_EXPANSION = 0.05
TIMESTEP = 0.2
SUBSTEP = 0.3
GRAVITY = 1.0

AXES = ("gx", "gy", "ga")
FIELDS = 6
FLUX_LANE = 40
FIELD_LANE = 80
VMEM_BYTES = 48 * 1024 * 1024


def lanes_of(shape):
    return lax.broadcasted_iota(jnp.int32, shape, len(shape) - 1)


def rows_of(shape):
    return lax.broadcasted_iota(jnp.int32, shape, len(shape) - 2)


def roll_lanes(x, amount):
    amount = amount % x.shape[-1] if isinstance(amount, int) else amount
    return x if isinstance(amount, int) and amount == 0 else pltpu.roll(x, amount, x.ndim - 1)


def roll_rows(x, amount):
    return pltpu.roll(x, amount % x.shape[-2], x.ndim - 2)


def coriolis_of(shape, row_start, total_rows):
    rows = (rows_of(shape) + row_start).astype(jnp.float32)
    return 0.3 + 0.4 * rows / total_rows


def edges_kernel(
    total_rows,
    thermal,
    current,
    surface,
    transport,
    flag,
    wet,
    to_west,
    to_east,
    to_north,
    to_south,
    packed,
    sums,
    loads,
):
    depth, ny, nx = thermal.shape
    shape = (ny, nx)
    lane = lanes_of(shape)
    row = rows_of(shape)
    levels = flag[...] * wet[...]
    zero = jnp.zeros(shape, jnp.float32)
    packed[...] = zero
    to_north[6 * W :, :] = jnp.zeros((to_north.shape[0] - 6 * W, nx), jnp.float32)
    to_south[6 * W :, :] = jnp.zeros((to_south.shape[0] - 6 * W, nx), jnp.float32)
    pad = -(-depth // 8) * 8
    p_row, f_row = 6 * W, 6 * W + pad
    for i in range(5):
        loads[i] = zero

    def level(k, carry):
        mask = levels > k
        t = jnp.where(mask, thermal[k], 0.0)
        u = current[0, k]
        v = current[1, k]
        loads[0] += jnp.where(mask, u, 0.0)
        loads[1] += jnp.where(mask, v, 0.0)
        p = loads[2] + t
        loads[2] = p
        east = u * t
        north = v * t
        ahead = jnp.where(lane == nx - 1, 0.0, roll_lanes(p, nx - 1))
        behind = jnp.where(lane == 0, 0.0, roll_lanes(p, 1))
        loads[3] += jnp.where(mask, ahead - behind, 0.0)
        above = jnp.where(row == ny - 1, 0.0, roll_rows(p, ny - 1))
        below = jnp.where(row == 0, 0.0, roll_rows(p, 1))
        loads[4] += jnp.where(mask, above - below, 0.0)
        pair = lane >> 1
        packed[...] = jnp.where(
            pair == k,
            roll_lanes(p, 2 * k + 1),
            jnp.where(pair == k + FLUX_LANE // 2, roll_lanes(east, FLUX_LANE + 2 * k + 1), packed[...]),
        )
        to_north[pl.ds(p_row + k, 1), :] = p[ny - 1 :]
        to_south[pl.ds(p_row + k, 1), :] = p[:1]
        to_north[pl.ds(f_row + k, 1), :] = north[ny - 1 :]
        to_south[pl.ds(f_row + k, 1), :] = north[:1]
        return carry

    lax.fori_loop(0, depth, level, 0)
    scale = TIMESTEP / depth
    slope = 0.5 * THERMAL_EXPANSION
    f = coriolis_of(shape, lax.axis_index("gy") * ny, total_rows)
    forcing_east = scale * (f * loads[1] - slope * loads[3])
    forcing_north = scale * (-f * loads[0] - slope * loads[4])
    sums[0] = loads[0]
    sums[1] = loads[1]
    sums[2] = forcing_east
    sums[3] = forcing_north
    fields = [
        surface[...],
        transport[0],
        transport[1],
        levels.astype(jnp.float32),
        forcing_east,
        forcing_north,
    ]
    pack = packed[...]
    west = roll_lanes(pack, nx - 1)
    east = roll_lanes(pack, 1)
    for i, field in enumerate(fields):
        place = FIELD_LANE + W * i
        mine = (lane >= place) & (lane < place + W)
        west = jnp.where(mine, roll_lanes(field, place), west)
        east = jnp.where(mine, roll_lanes(field, place - (nx - W)), east)
        to_north[W * i : W * (i + 1), :] = field[ny - W :]
        to_south[W * i : W * (i + 1), :] = field[:W]
    to_west[:ny, :] = west
    to_east[:ny, :] = east
    small = lanes_of((8, nx))
    west = jnp.zeros((8, nx), jnp.float32)
    east = west
    for side, ref in enumerate((to_south, to_north)):
        for group in range(pad // 8):
            place = pad * side + 8 * group
            mine = (small >= place) & (small < place + W)
            block = ref[p_row + 8 * group : p_row + 8 * (group + 1), :]
            west = jnp.where(mine, roll_lanes(block, place), west)
            east = jnp.where(mine, roll_lanes(block, place - (nx - W)), east)
    to_west[ny:, :] = west
    to_east[ny:, :] = east
    base = f_row + pad
    to_north[base:, :] = pack[ny - 8 :]
    to_south[base:, :] = pack[:8]


def column_sum(values, levels, parity):
    lane = lanes_of(values.shape)
    use = ((lane & 1) == parity) & (lane < FLUX_LANE) & ((lane >> 1).astype(jnp.float32) < levels)
    return jnp.sum(jnp.where(use, values, 0.0), axis=1, keepdims=True)


def row_sum(values, levels):
    use = rows_of(values.shape).astype(jnp.float32) < levels
    return jnp.sum(jnp.where(use, values, 0.0), axis=0, keepdims=True)


def unfold_rows(east_block, west_block, side, pad):
    nx = east_block.shape[1]
    lane = lanes_of(east_block.shape)
    out = []
    for group in range(pad // 8):
        place = pad * side + 8 * group
        out.append(
            jnp.where(
                lane < W,
                roll_lanes(east_block, -place),
                jnp.where(lane >= nx - W, roll_lanes(west_block, nx - W - place), 0.0),
            )
        )
    return jnp.concatenate(out, axis=0)


def subcycles(surface, transport, levels, sums, packed, from_west, from_east, from_south, from_north, own_north, own_south, pad):
    ny, nx = surface.shape
    p_row = 6 * W
    base = p_row + 2 * pad + 8
    west = jnp.concatenate([from_south[base : base + 8], from_west[:ny], from_north[base : base + 8]], axis=0)
    east = jnp.concatenate([from_south[base + 16 : base + 24], from_east[:ny], from_north[base + 16 : base + 24]], axis=0)
    mine = jnp.concatenate([from_south[base - 8 : base], packed, from_north[base - 8 : base]], axis=0)
    lane = lanes_of(west.shape)
    row = rows_of(west.shape)
    centres = []
    halos = []
    for i, field in enumerate([surface, transport[0], transport[1], levels.astype(jnp.float32), sums[2], sums[3]]):
        place = FIELD_LANE + W * i
        centres.append(jnp.concatenate([from_south[W * i : W * (i + 1)], field, from_north[W * i : W * (i + 1)]], axis=0))
        halos.append(
            jnp.where(
                lane < W,
                roll_lanes(east, -place),
                jnp.where(lane >= nx - W, roll_lanes(west, nx - W - place), 0.0),
            )
        )
    depth_centre, depth_halo = centres[3], halos[3]
    share = TIMESTEP / 20.0 * 0.5 * THERMAL_EXPANSION
    centres[4] = (
        centres[4]
        - jnp.where(lane == nx - 1, share * column_sum(east, depth_centre[:, nx - 1 :], 0), 0.0)
        + jnp.where(lane == 0, share * column_sum(west, depth_centre[:, :1], 1), 0.0)
    )
    halos[4] = (
        halos[4]
        + jnp.where(lane == 0, share * column_sum(mine, depth_halo[:, :1], 0), 0.0)
        - jnp.where(lane == nx - 1, share * column_sum(mine, depth_halo[:, nx - 1 :], 1), 0.0)
    )
    north_beyond = (
        from_north[p_row : p_row + pad],
        unfold_rows(from_north[base + 24 : base + 32], from_north[base + 8 : base + 16], 0, pad),
    )
    south_beyond = (
        from_south[p_row : p_row + pad],
        unfold_rows(from_south[base + 24 : base + 32], from_south[base + 8 : base + 16], 1, pad),
    )
    north_edge = (own_north, unfold_rows(from_east[ny:], from_west[ny:], 1, pad))
    south_edge = (own_south, unfold_rows(from_east[ny:], from_west[ny:], 0, pad))
    for part, fields, depths in ((0, centres, depth_centre), (1, halos, depth_halo)):
        top, bottom = W + ny - 1, W
        fields[5] = (
            fields[5]
            - jnp.where(row == top, share * row_sum(north_beyond[part], depths[top : top + 1]), 0.0)
            + jnp.where(row == bottom, share * row_sum(south_beyond[part], depths[bottom : bottom + 1]), 0.0)
            + jnp.where(row == top + 1, share * row_sum(north_edge[part], depths[top + 1 : top + 2]), 0.0)
            - jnp.where(row == bottom - 1, share * row_sum(south_edge[part], depths[bottom - 1 : bottom]), 0.0)
        )
    height, east_bar, north_bar, water, force_east, force_north = [
        jnp.concatenate([c, h], axis=1) for c, h in zip(centres, halos)
    ]
    wetness = jnp.where(water > 0.0, 1.0, 0.0)
    pull = (0.5 * SUBSTEP * GRAVITY / 20.0) * water
    push_east = SUBSTEP * wetness * force_east
    push_north = SUBSTEP * wetness * force_north
    spread = 0.5 * SUBSTEP * wetness
    cells, lines = height.shape[1], height.shape[0]
    for _ in range(NSUB):
        east_bar = wetness * east_bar + push_east - pull * (roll_lanes(height, cells - 1) - roll_lanes(height, 1))
        north_bar = wetness * north_bar + push_north - pull * (roll_rows(height, lines - 1) - roll_rows(height, 1))
        height = height - spread * (
            (roll_lanes(east_bar, cells - 1) - roll_lanes(east_bar, 1))
            + (roll_rows(north_bar, lines - 1) - roll_rows(north_bar, 1))
        )
    inner = slice(W, W + ny)
    return (
        height[inner, :nx],
        east_bar[inner, :nx],
        north_bar[inner, :nx],
        centres[4][inner],
        centres[5][inner],
    )


def finish_kernel(
    total_rows,
    thermal,
    current,
    mixing,
    surface,
    transport,
    flag,
    wet,
    sums,
    packed,
    own_north,
    own_south,
    from_west,
    from_east,
    from_south,
    from_north,
    mixed,
    velocity,
    height_out,
    transport_out,
    ratios,
    values,
    planes,
):
    depth, ny, nx = thermal.shape
    shape = (ny, nx)
    pad = -(-depth // 8) * 8
    p_row, f_row = 6 * W, 6 * W + pad
    levels = flag[...] * wet[...]
    height, east_bar, north_bar, force_east, force_north = subcycles(
        surface[...],
        (transport[0], transport[1]),
        levels,
        (sums[0], sums[1], sums[2], sums[3]),
        packed[...],
        from_west[...],
        from_east[...],
        from_south[...],
        from_north[...],
        own_north[p_row : p_row + pad],
        own_south[p_row : p_row + pad],
        pad,
    )
    height_out[...] = height
    transport_out[0] = east_bar
    transport_out[1] = north_bar
    count = jnp.maximum(levels.astype(jnp.float32), 1.0)
    planes[0] = east_bar - (sums[0] + depth * force_east) / count
    planes[1] = north_bar - (sums[1] + depth * force_north) / count
    lane = lanes_of(shape)
    row = rows_of(shape)
    planes[2] = jnp.where((lane & 1) == 0, from_east[:ny], from_west[:ny])
    planes[3] = jnp.zeros(shape, jnp.float32)
    planes[4] = TIMESTEP * coriolis_of(shape, lax.axis_index("gy") * ny, total_rows)
    slope = 0.5 * TIMESTEP * THERMAL_EXPANSION

    def ahead_less_behind(x, halo):
        return jnp.where(lane == nx - 1, halo, roll_lanes(x, nx - 1)) - jnp.where(lane == 0, halo, roll_lanes(x, 1))

    def above_less_below(x, above, below):
        return jnp.where(row == ny - 1, above, roll_rows(x, ny - 1)) - jnp.where(row == 0, below, roll_rows(x, 1))

    def forward(k, carry):
        mask = levels > k
        raw = thermal[k]
        t = jnp.where(mask, raw, 0.0)
        u = current[0, k]
        v = current[1, k]
        p = planes[3] + t
        planes[3] = p
        dx = ahead_less_behind(p, roll_lanes(planes[2], nx - 1 - 2 * k))
        dy = above_less_below(p, from_north[pl.ds(p_row + k, 1), :], from_south[pl.ds(p_row + k, 1), :])
        turn = planes[4]
        velocity[0, k] = jnp.where(mask, u + turn * v - slope * dx + planes[0], 0.0)
        velocity[1, k] = jnp.where(mask, v - turn * u - slope * dy + planes[1], 0.0)
        spread = ahead_less_behind(u * t, roll_lanes(planes[2], nx - 1 - FLUX_LANE - 2 * k)) + above_less_below(
            v * t, from_north[pl.ds(f_row + k, 1), :], from_south[pl.ds(f_row + k, 1), :]
        )
        source = jnp.where(mask, raw - 0.5 * TRANSPORT_SPEED * spread, 0.0)
        below = jnp.minimum(k + 1, depth - 1)
        upper = jnp.where((levels > k + 1) & (k < depth - 1), 0.5 * MIXING * (mixing[k] + mixing[below]), 0.0)
        lower = planes[5]
        planes[5] = upper
        above = jnp.maximum(k - 1, 0)
        inverse = 1.0 / (1.0 + upper + lower * (1.0 + ratios[above]))
        ratios[k] = -upper * inverse
        values[k] = (source + lower * values[above]) * inverse
        return carry

    planes[5] = jnp.zeros(shape, jnp.float32)
    ratios[0] = jnp.zeros(shape, jnp.float32)
    values[0] = jnp.zeros(shape, jnp.float32)
    lax.fori_loop(0, depth, forward, 0)
    mixed[depth - 1] = values[depth - 1]

    def backward(i, carry):
        k = depth - 2 - i
        mixed[k] = values[k] - ratios[k] * mixed[k + 1]
        return carry

    lax.fori_loop(0, depth - 1, backward, 0)


def shift(block, dx, dy):
    sx, sy, sa = (lax.axis_size(a) for a in AXES)
    pairs = []
    for x in range(sx * sa):
        for y in range(sy):
            tx, ty = (x + dx) % (sx * sa), y + dy
            if 0 <= ty < sy:
                source = (x // sa * sy + y) * sa + x % sa
                pairs.append((source, (tx // sa * sy + ty) * sa + tx % sa))
    return lax.ppermute(block, AXES, pairs)


def per_device(thermal, current, mixing, surface, transport, flag, wet):
    depth, ny, nx = thermal.shape
    total_rows = ny * lax.axis_size("gy")
    pad = -(-depth // 8) * 8
    f32 = jnp.float32
    whole = pl.BlockSpec(memory_space=pltpu.VMEM)
    params = pltpu.CompilerParams(vmem_limit_bytes=VMEM_BYTES)
    rows = 6 * W + 2 * pad + 8
    to_west, to_east, to_north, to_south, packed, sums = pl.pallas_call(
        functools.partial(edges_kernel, total_rows),
        out_shape=[
            jax.ShapeDtypeStruct((ny + 8, nx), f32),
            jax.ShapeDtypeStruct((ny + 8, nx), f32),
            jax.ShapeDtypeStruct((rows, nx), f32),
            jax.ShapeDtypeStruct((rows, nx), f32),
            jax.ShapeDtypeStruct((ny, nx), f32),
            jax.ShapeDtypeStruct((4, ny, nx), f32),
        ],
        in_specs=[whole] * 6,
        out_specs=[whole] * 6,
        scratch_shapes=[pltpu.VMEM((5, ny, nx), f32)],
        compiler_params=params,
        name="edges",
    )(thermal, current, surface, transport, flag, wet)
    from_west = shift(to_east, 1, 0)
    from_east = shift(to_west, -1, 0)
    north = jnp.concatenate([to_north, from_west[ny - 8 :], from_east[ny - 8 :]], axis=0)
    south = jnp.concatenate([to_south, from_west[:8], from_west[ny:], from_east[:8], from_east[ny:]], axis=0)
    from_south = shift(north, 0, 1)
    from_north = shift(south, 0, -1)
    return pl.pallas_call(
        functools.partial(finish_kernel, total_rows),
        out_shape=[
            jax.ShapeDtypeStruct((depth, ny, nx), f32),
            jax.ShapeDtypeStruct((2, depth, ny, nx), f32),
            jax.ShapeDtypeStruct((ny, nx), f32),
            jax.ShapeDtypeStruct((2, ny, nx), f32),
        ],
        in_specs=[whole] * 15,
        out_specs=[whole] * 4,
        scratch_shapes=[
            pltpu.VMEM((depth, ny, nx), f32),
            pltpu.VMEM((depth, ny, nx), f32),
            pltpu.VMEM((6, ny, nx), f32),
        ],
        compiler_params=params,
        name="finish",
    )(
        thermal,
        current,
        mixing,
        surface,
        transport,
        flag,
        wet,
        sums,
        packed,
        to_north,
        to_south,
        from_west,
        from_east,
        from_south,
        from_north,
    )


def solution(mesh):
    placed = (
        P(None, "gy", ("gx", "ga")),
        P(None, None, "gy", ("gx", "ga")),
        P(None, "gy", ("gx", "ga")),
        P("gy", ("gx", "ga")),
        P(None, "gy", ("gx", "ga")),
        P("gy", ("gx", "ga")),
        P("gy", ("gx", "ga")),
    )
    return jax.shard_map(
        per_device,
        mesh=mesh,
        in_specs=placed,
        out_specs=(
            P(None, "gy", ("gx", "ga")),
            P(None, None, "gy", ("gx", "ga")),
            P("gy", ("gx", "ga")),
            P(None, "gy", ("gx", "ga")),
        ),
        check_vma=False,
    )
```

```python
import functools

import jax
import jax.numpy as jnp
from jax import lax
from jax.experimental import pallas as pl
from jax.experimental.pallas import tpu as pltpu
from jax.sharding import PartitionSpec as P

NSUB = 4
W = 8
TRANSPORT_SPEED = 0.2
MIXING = 1.0
THERMAL_EXPANSION = 0.05
TIMESTEP = 0.2
SUBSTEP = 0.3
GRAVITY = 1.0

AXES = ("gx", "gy", "ga")
FIELDS = 6
FLUX_LANE = 20
FIELD_LANE = 40
FOLD_LANE = 88
FOLD = 30
FOLD_ROWS = 32
GROUPS = 4
UNROLL = 5
BACK_UNROLL = 4
VMEM_BYTES = 24 * 1024 * 1024
EDGES_VMEM = 54608 * 1024
COLUMNS_VMEM = 46 * 1024 * 1024


def lanes_of(shape):
    return lax.broadcasted_iota(jnp.int32, shape, len(shape) - 1)


def rows_of(shape):
    return lax.broadcasted_iota(jnp.int32, shape, len(shape) - 2)


def roll_lanes(x, amount):
    amount = amount % x.shape[-1] if isinstance(amount, int) else amount
    return x if isinstance(amount, int) and amount == 0 else pltpu.roll(x, amount, x.ndim - 1)


def roll_rows(x, amount):
    return pltpu.roll(x, amount % x.shape[-2], x.ndim - 2)


def coriolis_of(shape, row_start, total_rows):
    rows = (rows_of(shape) + row_start).astype(jnp.float32)
    return 0.3 + 0.4 * rows / total_rows


def fold(full):
    ny, nx = full.shape
    lane = lanes_of((FOLD_ROWS, nx))
    low = (ny - FOLD_ROWS) // 2
    middle = full[low : low + FOLD_ROWS]
    rest = jnp.concatenate([full[:low], full[low + FOLD_ROWS :]], axis=0)
    out = []
    for piece in range(3):
        part = rest[FOLD_ROWS * piece : FOLD_ROWS * (piece + 1)]
        out.append(jnp.where(lane < FOLD_LANE, part, roll_lanes(middle, FOLD_LANE - FOLD * piece)))
    return jnp.concatenate(out, axis=0)


def unfold(folded):
    rows, nx = folded.shape
    lane = lanes_of((FOLD_ROWS, nx))
    middle = jnp.zeros((FOLD_ROWS, nx), jnp.float32)
    for piece in range(3):
        part = folded[FOLD_ROWS * piece : FOLD_ROWS * (piece + 1)]
        mine = (lane >= FOLD * piece) & (lane < FOLD * (piece + 1))
        middle = jnp.where(mine, roll_lanes(part, FOLD * piece - FOLD_LANE), middle)
    return jnp.concatenate([folded[: rows // 2], middle, folded[rows // 2 :]], axis=0)


def edges_kernel(
    total_rows,
    thermal,
    current,
    surface,
    transport,
    flag,
    wet,
    first,
    second,
    to_first,
    to_second,
    packed,
    levels_here,
    sum_east,
    sum_north,
    force_east,
    force_north,
    ground,
    thermal_here,
    current_here,
    bars_here,
    edge_rows,
    packs,
    flag_here,
    wet_here,
    sems,
):
    depth, ny, nx = thermal.shape
    shape = (ny, nx)
    pad = -(-depth // 8) * 8
    step = depth // GROUPS
    masks = [
        pltpu.make_async_copy(flag, flag_here, sems.at[0]),
        pltpu.make_async_copy(wet, wet_here, sems.at[1]),
    ]
    slabs = []
    for g in range(GROUPS):
        part = pl.ds(g * step, step)
        slabs.append(
            [
                pltpu.make_async_copy(thermal.at[part], thermal_here.at[part], sems.at[3 + 3 * g]),
                pltpu.make_async_copy(current.at[0, part], current_here.at[0, part], sems.at[4 + 3 * g]),
                pltpu.make_async_copy(current.at[1, part], current_here.at[1, part], sems.at[5 + 3 * g]),
            ]
        )
    bars = [
        pltpu.make_async_copy(surface, bars_here.at[0], sems.at[3 + 3 * GROUPS]),
        pltpu.make_async_copy(transport, bars_here.at[pl.ds(1, 2)], sems.at[4 + 3 * GROUPS]),
    ]
    for copy in masks + [c for slab in slabs for c in slab] + bars:
        copy.start()
    lane = lanes_of(shape)
    zero = jnp.zeros(shape, jnp.float32)
    packs[0] = zero
    packs[1] = zero
    for ref in (sum_east, sum_north, force_east, force_north):
        ref[...] = zero
    edge_rows[...] = jnp.zeros(edge_rows.shape, jnp.float32)
    for copy in masks:
        copy.wait()
    levels_here[...] = (flag_here[...] * wet_here[...]).astype(jnp.float32)
    floor = pltpu.make_async_copy(levels_here, ground.at[0], sems.at[2])
    floor.start()

    def level(k, carry):
        weight = jnp.maximum(levels_here[...] - lax.convert_element_type(k, jnp.float32), 0.0)
        mask = weight > 0.0
        t = jnp.where(mask, thermal_here[k], 0.0)
        u = current_here[0, k]
        v = current_here[1, k]
        sum_east[...] += jnp.where(mask, u, 0.0)
        sum_north[...] += jnp.where(mask, v, 0.0)
        force_east[...] += weight * (roll_lanes(t, nx - 1) - roll_lanes(t, 1))
        force_north[...] += weight * (roll_rows(t, ny - 1) - roll_rows(t, 1))
        moved = roll_lanes(t, k + 1)
        flux = roll_lanes(u * t, FLUX_LANE + k + 1)
        packs[0] = jnp.where(lane == k, moved, jnp.where(lane == FLUX_LANE + k, flux, packs[0]))
        packs[1] = jnp.where(lane == k + 1, moved, jnp.where(lane == FLUX_LANE + k + 1, flux, packs[1]))
        edge_rows[0, pl.ds(k, 1), :] = t[:1]
        edge_rows[0, pl.ds(pad + k, 1), :] = v[:1] * t[:1]
        edge_rows[1, pl.ds(k, 1), :] = t[ny - 1 :]
        edge_rows[1, pl.ds(pad + k, 1), :] = v[ny - 1 :] * t[ny - 1 :]
        return carry

    for g in range(GROUPS):
        for copy in slabs[g]:
            copy.wait()
        lax.fori_loop(g * step, (g + 1) * step, level, 0, unroll=UNROLL)
    for copy in bars:
        copy.wait()
    levels = levels_here[...]
    row = rows_of(shape)
    east = packs[0]
    west = roll_lanes(packs[1], nx - 1)
    own = jnp.where(lane < FLUX_LANE, east, roll_lanes(west, FLUX_LANE))
    packed[...] = own
    zonal = (
        force_east[...]
        - jnp.where(lane == nx - 1, column_sum(west, levels[:, nx - 1 :], 0), 0.0)
        + jnp.where(lane == 0, column_sum(east, levels[:, :1], 0), 0.0)
    )
    merid = (
        force_north[...]
        - jnp.where(row == ny - 1, row_sum(edge_rows[0, :pad], levels[ny - 1 :]), 0.0)
        + jnp.where(row == 0, row_sum(edge_rows[1, :pad], levels[:1]), 0.0)
    )
    scale = TIMESTEP / depth
    slope = 0.5 * THERMAL_EXPANSION
    f = coriolis_of(shape, lax.axis_index("gy") * ny, total_rows)
    push_east = scale * (f * sum_north[...] - slope * zonal)
    push_north = scale * (-f * sum_east[...] - slope * merid)
    force_east[...] = push_east
    force_north[...] = push_north
    fields = [bars_here[0], bars_here[1], bars_here[2], levels, push_east, push_north]
    low = lax.axis_index("ga") == 0
    even = lax.axis_index("gy") % 2 == 0
    for i, field in enumerate(fields):
        place = FIELD_LANE + W * i
        mine = (lane >= place) & (lane < place + W)
        west = jnp.where(mine, roll_lanes(field, place), west)
        east = jnp.where(mine, roll_lanes(field, place - (nx - W)), east)
        to_first[W * i : W * (i + 1), :] = jnp.where(even, field[ny - W :], field[:W])
        to_second[W * i : W * (i + 1), :] = jnp.where(even, field[:W], field[ny - W :])
    east = fold(east)
    west = fold(west)
    tall = ny - FOLD_ROWS
    first[:tall, :] = jnp.where(low, east, west)
    second[:tall, :] = jnp.where(low, west, east)
    small = lanes_of((8, nx))
    west = jnp.zeros((8, nx), jnp.float32)
    east = west
    for side in (0, 1):
        for group in range(pad // 8):
            place = pad * side + 8 * group
            mine = (small >= place) & (small < place + W)
            block = edge_rows[side, 8 * group : 8 * (group + 1), :]
            west = jnp.where(mine, roll_lanes(block, place), west)
            east = jnp.where(mine, roll_lanes(block, place - (nx - W)), east)
    first[tall:, :] = jnp.where(low, east, west)
    second[tall:, :] = jnp.where(low, west, east)
    start = 6 * W
    base = start + 2 * pad
    to_first[start:base, :] = jnp.where(even, edge_rows[1], edge_rows[0])
    to_second[start:base, :] = jnp.where(even, edge_rows[0], edge_rows[1])
    to_first[base:, :] = jnp.where(even, own[ny - 8 :], own[:8])
    to_second[base:, :] = jnp.where(even, own[:8], own[ny - 8 :])
    floor.wait()


def column_sum(values, levels, place):
    lane = lanes_of(values.shape)
    use = (lane >= place) & (lane < place + FLUX_LANE)
    weight = jnp.maximum(levels - (lane - place).astype(jnp.float32), 0.0)
    return jnp.sum(jnp.where(use, weight * values, 0.0), axis=1, keepdims=True)


def row_sum(values, levels):
    weight = jnp.maximum(levels - rows_of(values.shape).astype(jnp.float32), 0.0)
    return jnp.sum(weight * values, axis=0, keepdims=True)


def unfold_rows(east_block, west_block, side, pad):
    nx = east_block.shape[1]
    lane = lanes_of(east_block.shape)
    out = []
    for group in range(pad // 8):
        place = pad * side + 8 * group
        out.append(
            jnp.where(
                lane < W,
                roll_lanes(east_block, -place),
                jnp.where(lane >= nx - W, roll_lanes(west_block, nx - W - place), 0.0),
            )
        )
    return jnp.concatenate(out, axis=0)


def subcycles(fields, packed, from_west, from_east, from_south, from_north, own_north, own_south, pad):
    ny, nx = packed.shape
    p_row = 6 * W
    base = p_row + 2 * pad + 8
    tall = ny - FOLD_ROWS
    west = jnp.concatenate([from_south[base : base + 8], unfold(from_west[:tall]), from_north[base : base + 8]], axis=0)
    east = jnp.concatenate([from_south[base + 16 : base + 24], unfold(from_east[:tall]), from_north[base + 16 : base + 24]], axis=0)
    mine = jnp.concatenate([from_south[base - 8 : base], packed, from_north[base - 8 : base]], axis=0)
    lane = lanes_of(west.shape)
    row = rows_of(west.shape)
    centres = []
    halos = []
    for i, field in enumerate(fields):
        place = FIELD_LANE + W * i
        centres.append(jnp.concatenate([from_south[W * i : W * (i + 1)], field, from_north[W * i : W * (i + 1)]], axis=0))
        halos.append(
            jnp.where(
                lane < W,
                roll_lanes(east, -place),
                jnp.where(lane >= nx - W, roll_lanes(west, nx - W - place), 0.0),
            )
        )
    depth_centre, depth_halo = centres[3], halos[3]
    share = TIMESTEP / 20.0 * 0.5 * THERMAL_EXPANSION
    centres[4] = (
        centres[4]
        - jnp.where(lane == nx - 1, share * column_sum(east, depth_centre[:, nx - 1 :], 0), 0.0)
        + jnp.where(lane == 0, share * column_sum(west, depth_centre[:, :1], 0), 0.0)
    )
    halos[4] = (
        halos[4]
        + jnp.where(lane == 0, share * column_sum(mine, depth_halo[:, :1], 0), 0.0)
        - jnp.where(lane == nx - 1, share * column_sum(mine, depth_halo[:, nx - 1 :], FLUX_LANE), 0.0)
    )
    north_beyond = (
        from_north[p_row : p_row + pad],
        unfold_rows(from_north[base + 24 : base + 32], from_north[base + 8 : base + 16], 0, pad),
    )
    south_beyond = (
        from_south[p_row : p_row + pad],
        unfold_rows(from_south[base + 24 : base + 32], from_south[base + 8 : base + 16], 1, pad),
    )
    north_edge = (own_north, unfold_rows(from_east[tall:], from_west[tall:], 1, pad))
    south_edge = (own_south, unfold_rows(from_east[tall:], from_west[tall:], 0, pad))
    for part, fields, depths in ((0, centres, depth_centre), (1, halos, depth_halo)):
        top, bottom = W + ny - 1, W
        fields[5] = (
            fields[5]
            - jnp.where(row == top, share * row_sum(north_beyond[part], depths[top : top + 1]), 0.0)
            + jnp.where(row == bottom, share * row_sum(south_beyond[part], depths[bottom : bottom + 1]), 0.0)
            + jnp.where(row == top + 1, share * row_sum(north_edge[part], depths[top + 1 : top + 2]), 0.0)
            - jnp.where(row == bottom - 1, share * row_sum(south_edge[part], depths[bottom - 1 : bottom]), 0.0)
        )
    height, east_bar, north_bar, water, force_east, force_north = [
        jnp.concatenate([c, h], axis=1) for c, h in zip(centres, halos)
    ]
    wetness = jnp.where(water > 0.0, 1.0, 0.0)
    pull = (0.5 * SUBSTEP * GRAVITY / 20.0) * water
    push_east = SUBSTEP * wetness * force_east
    push_north = SUBSTEP * wetness * force_north
    spread = 0.5 * SUBSTEP * wetness
    cells, lines = height.shape[1], height.shape[0]
    for _ in range(NSUB):
        east_bar = wetness * east_bar + push_east - pull * (roll_lanes(height, cells - 1) - roll_lanes(height, 1))
        north_bar = wetness * north_bar + push_north - pull * (roll_rows(height, lines - 1) - roll_rows(height, 1))
        height = height - spread * (
            (roll_lanes(east_bar, cells - 1) - roll_lanes(east_bar, 1))
            + (roll_rows(north_bar, lines - 1) - roll_rows(north_bar, 1))
        )
    inner = slice(W, W + ny)
    return (
        height[inner, :nx],
        east_bar[inner, :nx],
        north_bar[inner, :nx],
        centres[4][inner],
        centres[5][inner],
    )


def ahead_less_behind(x):
    lane = lanes_of(x.shape)
    nx = x.shape[1]
    return jnp.where(lane == nx - 1, 0.0, roll_lanes(x, nx - 1)) - jnp.where(lane == 0, 0.0, roll_lanes(x, 1))


def above_less_below(x):
    row = rows_of(x.shape)
    ny = x.shape[0]
    return jnp.where(row == ny - 1, 0.0, roll_rows(x, ny - 1)) - jnp.where(row == 0, 0.0, roll_rows(x, 1))


def columns_kernel(
    total_rows,
    thermal,
    current,
    mixing,
    ground,
    velocity_east,
    velocity_north,
    mixed,
    ratios,
    inverses,
    lowers,
    planes,
    levels,
    thermal_here,
    current_here,
    mixing_here,
    sems,
):
    depth, ny, nx = thermal.shape
    shape = (ny, nx)
    step = depth // GROUPS
    floor = pltpu.make_async_copy(ground.at[0], levels, sems.at[0])
    floor.start()
    slabs = []
    for g in range(GROUPS):
        part = pl.ds(g * step, step)
        more = pl.ds(g * step, step + 1) if g == 0 else pl.ds(g * step + 1, min(step, depth - g * step - 1))
        slabs.append(
            [
                pltpu.make_async_copy(thermal.at[part], thermal_here.at[part], sems.at[1 + 3 * g]),
                pltpu.make_async_copy(current.at[:, part], current_here.at[:, part], sems.at[2 + 3 * g]),
                pltpu.make_async_copy(mixing.at[more], mixing_here.at[more], sems.at[3 + 3 * g]),
            ]
        )
        for copy in slabs[-1]:
            copy.start()
    zero = jnp.zeros(shape, jnp.float32)
    planes[0] = zero
    planes[1] = zero
    planes[2] = zero
    planes[3] = TIMESTEP * coriolis_of(shape, lax.axis_index("gy") * ny, total_rows)
    ratios[0] = zero
    mixed[0] = zero
    slope = 0.5 * TIMESTEP * THERMAL_EXPANSION
    floor.wait()

    def forward(k, carry):
        wet = levels[...]
        mask = wet > lax.convert_element_type(k, jnp.float32)
        raw = thermal_here[k]
        t = jnp.where(mask, raw, 0.0)
        u = current_here[0, k]
        v = current_here[1, k]
        dx = planes[0] + slope * ahead_less_behind(t)
        dy = planes[1] + slope * above_less_below(t)
        planes[0] = dx
        planes[1] = dy
        turn = planes[3]
        velocity_east[k] = u + turn * v - dx
        velocity_north[k] = v - turn * u - dy
        spread = ahead_less_behind(u * t) + above_less_below(v * t)
        source = jnp.where(mask, raw - 0.5 * TRANSPORT_SPEED * spread, 0.0)
        below = jnp.minimum(k + 1, depth - 1)
        upper = jnp.where(
            wet > lax.convert_element_type(k + 1, jnp.float32), 0.5 * MIXING * (mixing_here[k] + mixing_here[below]), 0.0
        )
        lower = planes[2]
        planes[2] = upper
        above = jnp.maximum(k - 1, 0)
        inverse = 1.0 / (1.0 + upper + lower * (1.0 + ratios[above]))
        lower = lower * inverse
        inverses[k] = inverse
        lowers[k] = lower
        ratios[k] = -upper * inverse
        mixed[k] = source * inverse + lower * mixed[above]
        return carry

    for g in range(GROUPS):
        for copy in slabs[g]:
            copy.wait()
        lax.fori_loop(g * step, (g + 1) * step, forward, 0, unroll=UNROLL)

    def backward(i, carry):
        k = depth - 2 - i
        mixed[k] = mixed[k] - ratios[k] * mixed[k + 1]
        return carry

    lax.fori_loop(0, depth - 1, backward, 0, unroll=BACK_UNROLL)


def zonal_kernel(levels, from_first, from_second, velocity, mixed, ratios, inverses, lowers, velocity_out, mixed_out, planes):
    depth, ny, nx = mixed.shape
    shape = (ny, nx)
    lane = lanes_of(shape)
    low = lax.axis_index("ga") == 0
    tall = ny - FOLD_ROWS
    from_east = unfold(jnp.where(low, from_first[:tall], from_second[:tall]))
    from_west = unfold(jnp.where(low, from_second[:tall], from_first[:tall]))
    spot = rows_of((nx, nx))
    place = lanes_of((nx, nx))
    spread_east = jnp.where((place == 2 * spot) & (spot < FIELD_LANE), 1.0, 0.0)
    spread_west = jnp.where((place == 2 * spot + 1) & (spot < FIELD_LANE), 1.0, 0.0)

    def spread(x, where):
        return jnp.dot(x, where, precision=lax.Precision.HIGHEST, preferred_element_type=jnp.float32)

    halo = spread(from_west, spread_west) - spread(from_east, spread_east)
    slope = 0.5 * TIMESTEP * THERMAL_EXPANSION
    planes[0] = jnp.where(lane < 2 * FLUX_LANE, slope, 0.5 * TRANSPORT_SPEED) * halo
    zero = jnp.zeros(shape, jnp.float32)
    planes[1] = zero
    mixed_out[0] = zero

    def forward(k, carry):
        edge = (lane == 0) | (lane == nx - 1)
        mask = edge & (levels[...] > lax.convert_element_type(k, jnp.float32))
        push = planes[1] + jnp.where(edge, roll_lanes(planes[0], nx - 1 - 2 * k), 0.0)
        planes[1] = push
        velocity_out[k] = velocity[k] + push
        source = jnp.where(mask, roll_lanes(planes[0], nx - 1 - 2 * FLUX_LANE - 2 * k), 0.0)
        above = jnp.maximum(k - 1, 0)
        mixed_out[k] = source * inverses[k] + lowers[k] * mixed_out[above]
        return carry

    lax.fori_loop(0, depth, forward, 0, unroll=UNROLL)

    def backward(i, later):
        k = depth - 1 - i
        now = mixed_out[k] - ratios[k] * planes[1]
        planes[1] = now
        mixed_out[k] = mixed[k] + now
        return later

    planes[1] = zero
    lax.fori_loop(0, depth, backward, 0, unroll=BACK_UNROLL)


def finish_kernel(
    levels,
    surface,
    transport,
    sum_east,
    sum_north,
    push_east,
    push_north,
    packed,
    own_first,
    own_second,
    zonal_first,
    zonal_second,
    merid_first,
    merid_second,
    velocity_east,
    velocity_north,
    mixed,
    ratios,
    inverses,
    lowers,
    mixed_out,
    velocity_out,
    height_out,
    transport_out,
    velocity,
    rims,
    shallow,
    sems,
):
    depth, ny, nx = mixed.shape
    pad = -(-depth // 8) * 8
    p_row, f_row = 6 * W, 6 * W + pad
    middle = pltpu.make_async_copy(mixed.at[:, pl.ds(8, ny - 16)], mixed_out.at[:, pl.ds(8, ny - 16)], sems.at[0])
    middle.start()
    low = lax.axis_index("ga") == 0
    even = lax.axis_index("gy") % 2 == 0

    def choose(test, a, b):
        return jnp.where(test, a[...], b[...]), jnp.where(test, b[...], a[...])

    from_east, from_west = choose(low, zonal_first, zonal_second)
    from_north, from_south = choose(even, merid_first, merid_second)
    own_north, own_south = choose(even, own_first.at[pl.ds(p_row, pad)], own_second.at[pl.ds(p_row, pad)])
    base = f_row + pad + 8
    swapped = []
    for block in (from_north, from_south):
        one, two = block[base : base + 16], block[base + 16 : base + 32]
        swapped.append(
            jnp.concatenate([block[:base], jnp.where(low, two, one), jnp.where(low, one, two)], axis=0)
        )
    from_north, from_south = swapped

    slope = 0.5 * TIMESTEP * THERMAL_EXPANSION
    row = rows_of((8, nx))
    places = (0, ny - 8)
    parts = (row == 0, row == 7)
    signs = (1.0, -1.0)
    carried = [jnp.zeros((8, nx), jnp.float32) for _ in range(4)]
    pushes = [[], []]
    solved = [[], []]
    for k in range(depth):
        for s, block in enumerate((from_south, from_north)):
            place = pl.ds(places[s], 8)
            mask = parts[s] & (levels[place] > float(k))
            t = block[p_row + k : p_row + k + 1]
            flux = block[f_row + k : f_row + k + 1]
            carried[s] = carried[s] + jnp.where(parts[s], signs[s] * slope * t, 0.0)
            pushes[s].append(carried[s])
            source = jnp.where(mask, signs[s] * 0.5 * TRANSPORT_SPEED * flux, 0.0)
            carried[2 + s] = source * inverses[k, place] + lowers[k, place] * carried[2 + s]
            solved[s].append(carried[2 + s])
    for s in (0, 1):
        place = pl.ds(places[s], 8)
        later = jnp.zeros((8, nx), jnp.float32)
        for k in range(depth - 1, -1, -1):
            later = solved[s][k] - ratios[k, place] * later
            rims[0, k, pl.ds(8 * s, 8)] = mixed[k, place] + later
            rims[1, k, pl.ds(8 * s, 8)] = velocity_north[k, place] + pushes[s][k]
    edges = [
        pltpu.make_async_copy(rims.at[0, :, pl.ds(0, 8)], mixed_out.at[:, pl.ds(0, 8)], sems.at[1]),
        pltpu.make_async_copy(rims.at[0, :, pl.ds(8, 8)], mixed_out.at[:, pl.ds(ny - 8, 8)], sems.at[2]),
    ]
    for copy in edges:
        copy.start()

    fields = [surface[...], transport[0], transport[1], levels[...], push_east[...], push_north[...]]
    height, east_bar, north_bar, force_east, force_north = subcycles(
        fields, packed[...], from_west, from_east, from_south, from_north, own_north, own_south, pad
    )
    shallow[0] = height
    shallow[1] = east_bar
    shallow[2] = north_bar
    flat = [
        pltpu.make_async_copy(shallow.at[0], height_out, sems.at[3]),
        pltpu.make_async_copy(shallow.at[pl.ds(1, 2)], transport_out, sems.at[4]),
    ]
    for copy in flat:
        copy.start()
    count = jnp.maximum(levels[...], 1.0)
    shallow[3] = east_bar - (sum_east[...] + depth * force_east) / count
    shallow[4] = north_bar - (sum_north[...] + depth * force_north) / count

    def level(k, carry):
        mask = levels[...] > lax.convert_element_type(k, jnp.float32)
        velocity[0, k] = jnp.where(mask, velocity_east[k] + shallow[3], 0.0)
        velocity[1, k, 8 : ny - 8] = jnp.where(
            mask[8 : ny - 8], velocity_north[k, 8 : ny - 8] + shallow[4, 8 : ny - 8], 0.0
        )
        velocity[1, k, :8] = jnp.where(mask[:8], rims[1, k, :8] + shallow[4, :8], 0.0)
        velocity[1, k, ny - 8 :] = jnp.where(mask[ny - 8 :], rims[1, k, 8:] + shallow[4, ny - 8 :], 0.0)
        return carry

    step = depth // GROUPS
    slabs = []
    for g in range(GROUPS):
        lax.fori_loop(g * step, (g + 1) * step, level, 0, unroll=UNROLL)
        part = pl.ds(g * step, step)
        copy = pltpu.make_async_copy(velocity.at[:, part], velocity_out.at[:, part], sems.at[5 + g])
        copy.start()
        slabs.append(copy)
    for copy in [middle] + edges + flat + slabs:
        copy.wait()


def partner(block, zonal, parity):
    sx, sy, sa = (lax.axis_size(a) for a in AXES)
    count = sx * sa
    pairs = []
    for x in range(count):
        for y in range(sy):
            tx, ty = x, y
            if zonal:
                tx = (x + 1 if x % 2 == parity else x - 1) % count
            else:
                ty = y + 1 if y % 2 == parity else y - 1
            if 0 <= ty < sy:
                source = (x // sa * sy + y) * sa + x % sa
                pairs.append((source, (tx // sa * sy + ty) * sa + tx % sa))
    return lax.ppermute(block, AXES, pairs)


def estimate(flops, moved):
    return pl.CostEstimate(flops=flops, bytes_accessed=moved, transcendentals=0)


def per_device(thermal, current, mixing, surface, transport, flag, wet):
    depth, ny, nx = thermal.shape
    total_rows = ny * lax.axis_size("gy")
    pad = -(-depth // 8) * 8
    f32 = jnp.float32
    here = pl.BlockSpec(memory_space=pltpu.VMEM)
    far = pl.BlockSpec(memory_space=pltpu.HBM)
    params = pltpu.CompilerParams(vmem_limit_bytes=VMEM_BYTES)
    rows = 6 * W + 2 * pad + 8
    sd = jax.ShapeDtypeStruct
    cube = sd((depth, ny, nx), f32)
    pair = sd((2, depth, ny, nx), f32)
    cells = depth * ny * nx
    plane = sd((ny, nx), f32)
    edge = sd((ny - FOLD_ROWS + 8, nx), f32)
    outs = pl.pallas_call(
        functools.partial(edges_kernel, total_rows),
        out_shape=[edge, edge, sd((rows, nx), f32), sd((rows, nx), f32)] + [plane] * 6 + [sd((24, ny, nx), f32)],
        in_specs=[far] * 6,
        out_specs=[here] * 10 + [far],
        scratch_shapes=[
            pltpu.VMEM((depth, ny, nx), f32),
            pltpu.VMEM((2, depth, ny, nx), f32),
            pltpu.VMEM((3, ny, nx), f32),
            pltpu.VMEM((2, 2 * pad, nx), f32),
            pltpu.VMEM((2, ny, nx), f32),
            pltpu.VMEM((ny, nx), jnp.int32),
            pltpu.VMEM((ny, nx), jnp.int32),
            pltpu.SemaphoreType.DMA((5 + 3 * GROUPS,)),
        ],
        compiler_params=pltpu.CompilerParams(vmem_limit_bytes=EDGES_VMEM),
        cost_estimate=estimate(30 * cells, 12 * cells),
        name="edges",
    )(thermal, current, surface, transport, flag, wet)
    first, second, to_first, to_second, packed, levels, sum_east, sum_north, force_east, force_north, ground = outs
    zonal_first = partner(first, True, 0)
    zonal_second = partner(second, True, 1)
    velocity_east, velocity_north, mixed, ratios, inverses, lowers = pl.pallas_call(
        functools.partial(columns_kernel, total_rows),
        out_shape=[cube] * 6,
        in_specs=[far] * 4,
        out_specs=[here] * 6,
        scratch_shapes=[
            pltpu.VMEM((4, ny, nx), f32),
            pltpu.VMEM((ny, nx), f32),
            pltpu.VMEM((depth, ny, nx), f32),
            pltpu.VMEM((2, depth, ny, nx), f32),
            pltpu.VMEM((depth, ny, nx), f32),
            pltpu.SemaphoreType.DMA((1 + 3 * GROUPS,)),
        ],
        compiler_params=pltpu.CompilerParams(vmem_limit_bytes=COLUMNS_VMEM),
        cost_estimate=estimate(100 * cells, 40 * cells),
        name="columns",
    )(thermal, current, mixing, ground)
    zonal_first, zonal_second, velocity_east = lax.optimization_barrier((zonal_first, zonal_second, velocity_east))
    even = lax.axis_index("gy") % 2 == 0
    tall = ny - FOLD_ROWS
    top = [zonal_first[tall - 8 :], zonal_second[tall - 8 :]]
    bottom = [zonal_first[:8], zonal_first[tall:], zonal_second[:8], zonal_second[tall:]]
    top = jnp.concatenate(top, axis=0)
    bottom = jnp.concatenate(bottom, axis=0)
    merid_first = partner(jnp.concatenate([to_first, jnp.where(even, top, bottom)], axis=0), False, 0)
    merid_second = partner(jnp.concatenate([to_second, jnp.where(even, bottom, top)], axis=0), False, 1)
    velocity_east, mixed = pl.pallas_call(
        zonal_kernel,
        out_shape=[cube, cube],
        in_specs=[here] * 8,
        out_specs=[here] * 2,
        scratch_shapes=[pltpu.VMEM((2, ny, nx), f32)],
        compiler_params=params,
        cost_estimate=estimate(20 * cells, 20 * cells),
        name="zonal",
    )(levels, zonal_first, zonal_second, velocity_east, mixed, ratios, inverses, lowers)
    return pl.pallas_call(
        finish_kernel,
        out_shape=[cube, pair, sd((ny, nx), f32), sd((2, ny, nx), f32)],
        in_specs=[here] * 20,
        out_specs=[far] * 4,
        scratch_shapes=[
            pltpu.VMEM((2, depth, ny, nx), f32),
            pltpu.VMEM((2, depth, 16, nx), f32),
            pltpu.VMEM((5, ny, nx), f32),
            pltpu.SemaphoreType.DMA((5 + GROUPS,)),
        ],
        compiler_params=params,
        name="finish",
    )(
        levels,
        surface,
        transport,
        sum_east,
        sum_north,
        force_east,
        force_north,
        packed,
        to_first,
        to_second,
        zonal_first,
        zonal_second,
        merid_first,
        merid_second,
        velocity_east,
        velocity_north,
        mixed,
        ratios,
        inverses,
        lowers,
    )


def solution(mesh):
    placed = (
        P(None, "gy", ("gx", "ga")),
        P(None, None, "gy", ("gx", "ga")),
        P(None, "gy", ("gx", "ga")),
        P("gy", ("gx", "ga")),
        P(None, "gy", ("gx", "ga")),
        P("gy", ("gx", "ga")),
        P("gy", ("gx", "ga")),
    )
    return jax.shard_map(
        per_device,
        mesh=mesh,
        in_specs=placed,
        out_specs=(
            P(None, "gy", ("gx", "ga")),
            P(None, None, "gy", ("gx", "ga")),
            P("gy", ("gx", "ga")),
            P(None, "gy", ("gx", "ga")),
        ),
        check_vma=False,
    )
```

```python
import functools

import jax
import jax.numpy as jnp
from jax import lax
from jax.experimental import pallas as pl
from jax.experimental.pallas import tpu as pltpu
from jax.sharding import PartitionSpec as P

NSUB = 4
W = 8
TRANSPORT_SPEED = 0.2
MIXING = 1.0
THERMAL_EXPANSION = 0.05
TIMESTEP = 0.2
SUBSTEP = 0.3
GRAVITY = 1.0

AXES = ("gx", "gy", "ga")
FIELDS = 6
FLUX_LANE = 20
FIELD_LANE = 40
FOLD_LANE = 88
FOLD = 30
FOLD_ROWS = 32
GROUPS = 4
CHUNK = 32
SLABS = (4, 6, 6, 4)
UNROLL = 5
BACK_UNROLL = 4
VMEM_BYTES = 24 * 1024 * 1024
EDGES_VMEM = 54608 * 1024
COLUMNS_VMEM = 46 * 1024 * 1024


def lanes_of(shape):
    return lax.broadcasted_iota(jnp.int32, shape, len(shape) - 1)


def rows_of(shape):
    return lax.broadcasted_iota(jnp.int32, shape, len(shape) - 2)


def roll_lanes(x, amount):
    amount = amount % x.shape[-1] if isinstance(amount, int) else amount
    return x if isinstance(amount, int) and amount == 0 else pltpu.roll(x, amount, x.ndim - 1)


def roll_rows(x, amount):
    return pltpu.roll(x, amount % x.shape[-2], x.ndim - 2)


def coriolis_of(shape, row_start, total_rows):
    rows = (rows_of(shape) + row_start).astype(jnp.float32)
    return 0.3 + 0.4 * rows / total_rows


def fold(full):
    ny, nx = full.shape
    lane = lanes_of((FOLD_ROWS, nx))
    low = (ny - FOLD_ROWS) // 2
    middle = full[low : low + FOLD_ROWS]
    rest = jnp.concatenate([full[:low], full[low + FOLD_ROWS :]], axis=0)
    out = []
    for piece in range(3):
        part = rest[FOLD_ROWS * piece : FOLD_ROWS * (piece + 1)]
        out.append(jnp.where(lane < FOLD_LANE, part, roll_lanes(middle, FOLD_LANE - FOLD * piece)))
    return jnp.concatenate(out, axis=0)


def unfold(folded):
    rows, nx = folded.shape
    lane = lanes_of((FOLD_ROWS, nx))
    middle = jnp.zeros((FOLD_ROWS, nx), jnp.float32)
    for piece in range(3):
        part = folded[FOLD_ROWS * piece : FOLD_ROWS * (piece + 1)]
        mine = (lane >= FOLD * piece) & (lane < FOLD * (piece + 1))
        middle = jnp.where(mine, roll_lanes(part, FOLD * piece - FOLD_LANE), middle)
    return jnp.concatenate([folded[: rows // 2], middle, folded[rows // 2 :]], axis=0)


def edges_kernel(
    total_rows,
    thermal,
    current,
    surface,
    transport,
    flag,
    wet,
    first,
    second,
    to_first,
    to_second,
    packed,
    levels_here,
    sum_east,
    sum_north,
    force_east,
    force_north,
    ground,
    thermal_here,
    current_here,
    bars_here,
    edge_rows,
    packs,
    flag_here,
    wet_here,
    sems,
):
    depth, ny, nx = thermal.shape
    shape = (ny, nx)
    pad = -(-depth // 8) * 8
    masks = [
        pltpu.make_async_copy(flag, flag_here, sems.at[0]),
        pltpu.make_async_copy(wet, wet_here, sems.at[1]),
    ]
    slabs = []
    begin = 0
    for g, count in enumerate(SLABS):
        part = pl.ds(begin, count)
        begin += count
        slabs.append(
            [
                pltpu.make_async_copy(thermal.at[part], thermal_here.at[part], sems.at[3 + 3 * g]),
                pltpu.make_async_copy(current.at[0, part], current_here.at[0, part], sems.at[4 + 3 * g]),
                pltpu.make_async_copy(current.at[1, part], current_here.at[1, part], sems.at[5 + 3 * g]),
            ]
        )
    bars = [
        pltpu.make_async_copy(surface, bars_here.at[0], sems.at[3 + 3 * GROUPS]),
        pltpu.make_async_copy(transport, bars_here.at[pl.ds(1, 2)], sems.at[4 + 3 * GROUPS]),
    ]
    for copy in masks + [c for slab in slabs for c in slab] + bars:
        copy.start()
    lane = lanes_of(shape)
    zero = jnp.zeros(shape, jnp.float32)
    packs[0] = zero
    packs[1] = zero
    for ref in (sum_east, sum_north, force_east, force_north):
        ref[...] = zero
    edge_rows[...] = jnp.zeros(edge_rows.shape, jnp.float32)
    for copy in masks:
        copy.wait()
    levels_here[...] = (flag_here[...] * wet_here[...]).astype(jnp.float32)
    floor = pltpu.make_async_copy(levels_here, ground.at[0], sems.at[2])
    floor.start()

    def chunk(begin, count, start):
        inner = pl.ds(start, CHUNK)
        low, high = max(start - 8, 0), min(start + CHUNK + 8, ny)
        deep = levels_here[low:high]
        mine = slice(start - low, start - low + CHUNK)
        part = lanes_of((CHUNK, nx))
        row = rows_of((CHUNK, nx))
        totals = [ref[inner] for ref in (sum_east, sum_north, force_east, force_north)]
        east, west = packs[0, inner], packs[1, inner]
        for k in range(begin, begin + count):
            weight = jnp.maximum(deep[mine] - float(k), 0.0)
            mask = weight > 0.0
            wide = jnp.where(deep > float(k), thermal_here[k, low:high], 0.0)
            t = wide[mine]
            u = current_here[0, k, inner]
            v = current_here[1, k, inner]
            totals[0] += jnp.where(mask, u, 0.0)
            totals[1] += jnp.where(mask, v, 0.0)
            totals[2] += weight * (roll_lanes(t, nx - 1) - roll_lanes(t, 1))
            above = roll_rows(wide, -1)[mine]
            below = roll_rows(wide, 1)[mine]
            if high == ny:
                above = jnp.where(row == CHUNK - 1, 0.0, above)
            if low == 0:
                below = jnp.where(row == 0, 0.0, below)
            totals[3] += weight * (above - below)
            moved = roll_lanes(t, k + 1)
            flux = roll_lanes(u * t, FLUX_LANE + k + 1)
            east = jnp.where(part == k, moved, jnp.where(part == FLUX_LANE + k, flux, east))
            west = jnp.where(part == k + 1, moved, jnp.where(part == FLUX_LANE + k + 1, flux, west))
            if start == 0:
                edge_rows[0, k : k + 1, :] = t[:1]
                edge_rows[0, pad + k : pad + k + 1, :] = v[:1] * t[:1]
            if start == ny - CHUNK:
                edge_rows[1, k : k + 1, :] = t[CHUNK - 1 :]
                edge_rows[1, pad + k : pad + k + 1, :] = v[CHUNK - 1 :] * t[CHUNK - 1 :]
        for ref, total in zip((sum_east, sum_north, force_east, force_north), totals):
            ref[inner] = total
        packs[0, inner], packs[1, inner] = east, west

    begin = 0
    for slab, count in zip(slabs, SLABS):
        for copy in slab:
            copy.wait()
        for start in range(0, ny, CHUNK):
            chunk(begin, count, start)
        begin += count
    for copy in bars:
        copy.wait()
    levels = levels_here[...]
    east = packs[0]
    west = roll_lanes(packs[1], nx - 1)
    own = jnp.where(lane < FLUX_LANE, east, roll_lanes(west, FLUX_LANE))
    packed[...] = own
    zonal = (
        force_east[...]
        - jnp.where(lane == nx - 1, column_sum(west, levels[:, nx - 1 :], 0), 0.0)
        + jnp.where(lane == 0, column_sum(east, levels[:, :1], 0), 0.0)
    )
    scale = TIMESTEP / depth
    slope = 0.5 * THERMAL_EXPANSION
    f = coriolis_of(shape, lax.axis_index("gy") * ny, total_rows)
    push_east = scale * (f * sum_north[...] - slope * zonal)
    push_north = scale * (-f * sum_east[...] - slope * force_north[...])
    force_east[...] = push_east
    force_north[...] = push_north
    fields = [bars_here[0], bars_here[1], bars_here[2], levels, push_east, push_north]
    low = lax.axis_index("ga") == 0
    even = lax.axis_index("gy") % 2 == 0
    for i, field in enumerate(fields):
        place = FIELD_LANE + W * i
        mine = (lane >= place) & (lane < place + W)
        west = jnp.where(mine, roll_lanes(field, place), west)
        east = jnp.where(mine, roll_lanes(field, place - (nx - W)), east)
        to_first[W * i : W * (i + 1), :] = jnp.where(even, field[ny - W :], field[:W])
        to_second[W * i : W * (i + 1), :] = jnp.where(even, field[:W], field[ny - W :])
    east = fold(east)
    west = fold(west)
    tall = ny - FOLD_ROWS
    first[:tall, :] = jnp.where(low, east, west)
    second[:tall, :] = jnp.where(low, west, east)
    small = lanes_of((8, nx))
    west = jnp.zeros((8, nx), jnp.float32)
    east = west
    for side in (0, 1):
        for group in range(pad // 8):
            place = pad * side + 8 * group
            mine = (small >= place) & (small < place + W)
            block = edge_rows[side, 8 * group : 8 * (group + 1), :]
            west = jnp.where(mine, roll_lanes(block, place), west)
            east = jnp.where(mine, roll_lanes(block, place - (nx - W)), east)
    first[tall:, :] = jnp.where(low, east, west)
    second[tall:, :] = jnp.where(low, west, east)
    start = 6 * W
    base = start + 2 * pad
    to_first[start:base, :] = jnp.where(even, edge_rows[1], edge_rows[0])
    to_second[start:base, :] = jnp.where(even, edge_rows[0], edge_rows[1])
    to_first[base:, :] = jnp.where(even, own[ny - 8 :], own[:8])
    to_second[base:, :] = jnp.where(even, own[:8], own[ny - 8 :])
    floor.wait()


def column_sum(values, levels, place):
    lane = lanes_of(values.shape)
    use = (lane >= place) & (lane < place + FLUX_LANE)
    weight = jnp.maximum(levels - (lane - place).astype(jnp.float32), 0.0)
    return jnp.sum(jnp.where(use, weight * values, 0.0), axis=1, keepdims=True)


def row_sum(values, levels):
    weight = jnp.maximum(levels - rows_of(values.shape).astype(jnp.float32), 0.0)
    return jnp.sum(weight * values, axis=0, keepdims=True)


def unfold_rows(east_block, west_block, side, pad):
    nx = east_block.shape[1]
    lane = lanes_of(east_block.shape)
    out = []
    for group in range(pad // 8):
        place = pad * side + 8 * group
        out.append(
            jnp.where(
                lane < W,
                roll_lanes(east_block, -place),
                jnp.where(lane >= nx - W, roll_lanes(west_block, nx - W - place), 0.0),
            )
        )
    return jnp.concatenate(out, axis=0)


def subcycles(fields, packed, from_west, from_east, from_south, from_north, own_north, own_south, pad):
    ny, nx = packed.shape
    p_row = 6 * W
    base = p_row + 2 * pad + 8
    tall = ny - FOLD_ROWS
    west = jnp.concatenate([from_south[base : base + 8], unfold(from_west[:tall]), from_north[base : base + 8]], axis=0)
    east = jnp.concatenate([from_south[base + 16 : base + 24], unfold(from_east[:tall]), from_north[base + 16 : base + 24]], axis=0)
    mine = jnp.concatenate([from_south[base - 8 : base], packed, from_north[base - 8 : base]], axis=0)
    lane = lanes_of(west.shape)
    row = rows_of(west.shape)
    centres = []
    halos = []
    for i, field in enumerate(fields):
        place = FIELD_LANE + W * i
        centres.append(jnp.concatenate([from_south[W * i : W * (i + 1)], field, from_north[W * i : W * (i + 1)]], axis=0))
        halos.append(
            jnp.where(
                lane < W,
                roll_lanes(east, -place),
                jnp.where(lane >= nx - W, roll_lanes(west, nx - W - place), 0.0),
            )
        )
    depth_centre, depth_halo = centres[3], halos[3]
    share = TIMESTEP / 20.0 * 0.5 * THERMAL_EXPANSION
    centres[4] = (
        centres[4]
        - jnp.where(lane == nx - 1, share * column_sum(east, depth_centre[:, nx - 1 :], 0), 0.0)
        + jnp.where(lane == 0, share * column_sum(west, depth_centre[:, :1], 0), 0.0)
    )
    halos[4] = (
        halos[4]
        + jnp.where(lane == 0, share * column_sum(mine, depth_halo[:, :1], 0), 0.0)
        - jnp.where(lane == nx - 1, share * column_sum(mine, depth_halo[:, nx - 1 :], FLUX_LANE), 0.0)
    )
    north_beyond = (
        from_north[p_row : p_row + pad],
        unfold_rows(from_north[base + 24 : base + 32], from_north[base + 8 : base + 16], 0, pad),
    )
    south_beyond = (
        from_south[p_row : p_row + pad],
        unfold_rows(from_south[base + 24 : base + 32], from_south[base + 8 : base + 16], 1, pad),
    )
    north_edge = (own_north, unfold_rows(from_east[tall:], from_west[tall:], 1, pad))
    south_edge = (own_south, unfold_rows(from_east[tall:], from_west[tall:], 0, pad))
    for part, fields, depths in ((0, centres, depth_centre), (1, halos, depth_halo)):
        top, bottom = W + ny - 1, W
        fields[5] = (
            fields[5]
            - jnp.where(row == top, share * row_sum(north_beyond[part], depths[top : top + 1]), 0.0)
            + jnp.where(row == bottom, share * row_sum(south_beyond[part], depths[bottom : bottom + 1]), 0.0)
            + jnp.where(row == top + 1, share * row_sum(north_edge[part], depths[top + 1 : top + 2]), 0.0)
            - jnp.where(row == bottom - 1, share * row_sum(south_edge[part], depths[bottom - 1 : bottom]), 0.0)
        )
    height, east_bar, north_bar, water, force_east, force_north = [
        jnp.concatenate([c, h], axis=1) for c, h in zip(centres, halos)
    ]
    wetness = jnp.where(water > 0.0, 1.0, 0.0)
    pull = (0.5 * SUBSTEP * GRAVITY / 20.0) * water
    push_east = SUBSTEP * wetness * force_east
    push_north = SUBSTEP * wetness * force_north
    spread = 0.5 * SUBSTEP * wetness
    cells, lines = height.shape[1], height.shape[0]
    for _ in range(NSUB):
        east_bar = wetness * east_bar + push_east - pull * (roll_lanes(height, cells - 1) - roll_lanes(height, 1))
        north_bar = wetness * north_bar + push_north - pull * (roll_rows(height, lines - 1) - roll_rows(height, 1))
        height = height - spread * (
            (roll_lanes(east_bar, cells - 1) - roll_lanes(east_bar, 1))
            + (roll_rows(north_bar, lines - 1) - roll_rows(north_bar, 1))
        )
    inner = slice(W, W + ny)
    return (
        height[inner, :nx],
        east_bar[inner, :nx],
        north_bar[inner, :nx],
        centres[4][inner],
        centres[5][inner],
    )


def ahead_less_behind(x):
    lane = lanes_of(x.shape)
    nx = x.shape[1]
    return jnp.where(lane == nx - 1, 0.0, roll_lanes(x, nx - 1)) - jnp.where(lane == 0, 0.0, roll_lanes(x, 1))


def above_less_below(x):
    row = rows_of(x.shape)
    ny = x.shape[0]
    return jnp.where(row == ny - 1, 0.0, roll_rows(x, ny - 1)) - jnp.where(row == 0, 0.0, roll_rows(x, 1))


def columns_kernel(
    total_rows,
    thermal,
    current,
    mixing,
    ground,
    velocity_east,
    velocity_north,
    mixed,
    ratios,
    inverses,
    lowers,
    planes,
    levels,
    thermal_here,
    current_here,
    mixing_here,
    sems,
):
    depth, ny, nx = thermal.shape
    shape = (ny, nx)
    step = depth // GROUPS
    floor = pltpu.make_async_copy(ground.at[0], levels, sems.at[0])
    floor.start()
    slabs = []
    for g in range(GROUPS):
        part = pl.ds(g * step, step)
        more = pl.ds(g * step, step + 1) if g == 0 else pl.ds(g * step + 1, min(step, depth - g * step - 1))
        slabs.append(
            [
                pltpu.make_async_copy(thermal.at[part], thermal_here.at[part], sems.at[1 + 3 * g]),
                pltpu.make_async_copy(current.at[:, part], current_here.at[:, part], sems.at[2 + 3 * g]),
                pltpu.make_async_copy(mixing.at[more], mixing_here.at[more], sems.at[3 + 3 * g]),
            ]
        )
        for copy in slabs[-1]:
            copy.start()
    zero = jnp.zeros(shape, jnp.float32)
    planes[0] = zero
    planes[1] = zero
    planes[2] = zero
    planes[3] = TIMESTEP * coriolis_of(shape, lax.axis_index("gy") * ny, total_rows)
    ratios[0] = zero
    mixed[0] = zero
    slope = 0.5 * TIMESTEP * THERMAL_EXPANSION
    floor.wait()

    def forward(k, carry):
        wet = levels[...]
        mask = wet > lax.convert_element_type(k, jnp.float32)
        raw = thermal_here[k]
        t = jnp.where(mask, raw, 0.0)
        u = current_here[0, k]
        v = current_here[1, k]
        dx = planes[0] + slope * ahead_less_behind(t)
        dy = planes[1] + slope * above_less_below(t)
        planes[0] = dx
        planes[1] = dy
        turn = planes[3]
        velocity_east[k] = u + turn * v - dx
        velocity_north[k] = v - turn * u - dy
        spread = ahead_less_behind(u * t) + above_less_below(v * t)
        source = jnp.where(mask, raw - 0.5 * TRANSPORT_SPEED * spread, 0.0)
        below = jnp.minimum(k + 1, depth - 1)
        upper = jnp.where(
            wet > lax.convert_element_type(k + 1, jnp.float32), 0.5 * MIXING * (mixing_here[k] + mixing_here[below]), 0.0
        )
        lower = planes[2]
        planes[2] = upper
        above = jnp.maximum(k - 1, 0)
        inverse = 1.0 / (1.0 + upper + lower * (1.0 + ratios[above]))
        lower = lower * inverse
        inverses[k] = inverse
        lowers[k] = lower
        ratios[k] = -upper * inverse
        mixed[k] = source * inverse + lower * mixed[above]
        return carry

    for g in range(GROUPS):
        for copy in slabs[g]:
            copy.wait()
        lax.fori_loop(g * step, (g + 1) * step, forward, 0, unroll=UNROLL)

    def backward(i, carry):
        k = depth - 2 - i
        mixed[k] = mixed[k] - ratios[k] * mixed[k + 1]
        return carry

    lax.fori_loop(0, depth - 1, backward, 0, unroll=BACK_UNROLL)


def zonal_kernel(levels, from_first, from_second, velocity, mixed, ratios, inverses, lowers, velocity_out, mixed_out, planes):
    depth, ny, nx = mixed.shape
    shape = (ny, nx)
    lane = lanes_of(shape)
    low = lax.axis_index("ga") == 0
    tall = ny - FOLD_ROWS
    from_east = unfold(jnp.where(low, from_first[:tall], from_second[:tall]))
    from_west = unfold(jnp.where(low, from_second[:tall], from_first[:tall]))
    spot = rows_of((nx, nx))
    place = lanes_of((nx, nx))
    spread_east = jnp.where((place == 2 * spot) & (spot < FIELD_LANE), 1.0, 0.0)
    spread_west = jnp.where((place == 2 * spot + 1) & (spot < FIELD_LANE), 1.0, 0.0)

    def spread(x, where):
        return jnp.dot(x, where, precision=lax.Precision.HIGHEST, preferred_element_type=jnp.float32)

    halo = spread(from_west, spread_west) - spread(from_east, spread_east)
    slope = 0.5 * TIMESTEP * THERMAL_EXPANSION
    planes[0] = jnp.where(lane < 2 * FLUX_LANE, slope, 0.5 * TRANSPORT_SPEED) * halo
    zero = jnp.zeros(shape, jnp.float32)
    planes[1] = zero
    mixed_out[0] = zero

    def forward(k, carry):
        edge = (lane == 0) | (lane == nx - 1)
        mask = edge & (levels[...] > lax.convert_element_type(k, jnp.float32))
        push = planes[1] + jnp.where(edge, roll_lanes(planes[0], nx - 1 - 2 * k), 0.0)
        planes[1] = push
        velocity_out[k] = velocity[k] + push
        source = jnp.where(mask, roll_lanes(planes[0], nx - 1 - 2 * FLUX_LANE - 2 * k), 0.0)
        above = jnp.maximum(k - 1, 0)
        mixed_out[k] = source * inverses[k] + lowers[k] * mixed_out[above]
        return carry

    lax.fori_loop(0, depth, forward, 0, unroll=UNROLL)

    def backward(i, later):
        k = depth - 1 - i
        now = mixed_out[k] - ratios[k] * planes[1]
        planes[1] = now
        mixed_out[k] = mixed[k] + now
        return later

    planes[1] = zero
    lax.fori_loop(0, depth, backward, 0, unroll=BACK_UNROLL)


def finish_kernel(
    levels,
    surface,
    transport,
    sum_east,
    sum_north,
    push_east,
    push_north,
    packed,
    own_first,
    own_second,
    zonal_first,
    zonal_second,
    merid_second,
    merid_first,
    velocity_east,
    velocity_north,
    mixed,
    ratios,
    inverses,
    lowers,
    mixed_out,
    velocity_out,
    height_out,
    transport_out,
    velocity,
    rims,
    shallow,
    sems,
):
    depth, ny, nx = mixed.shape
    pad = -(-depth // 8) * 8
    p_row, f_row = 6 * W, 6 * W + pad
    middle = pltpu.make_async_copy(mixed.at[:, pl.ds(8, ny - 16)], mixed_out.at[:, pl.ds(8, ny - 16)], sems.at[0])
    middle.start()
    low = lax.axis_index("ga") == 0
    even = lax.axis_index("gy") % 2 == 0

    def choose(test, a, b):
        return jnp.where(test, a[...], b[...]), jnp.where(test, b[...], a[...])

    from_east, from_west = choose(low, zonal_first, zonal_second)
    from_north, from_south = choose(even, merid_first, merid_second)
    own_north, own_south = choose(even, own_first.at[pl.ds(p_row, pad)], own_second.at[pl.ds(p_row, pad)])
    base = f_row + pad + 8
    swapped = []
    for block in (from_north, from_south):
        one, two = block[base : base + 16], block[base + 16 : base + 32]
        swapped.append(
            jnp.concatenate([block[:base], jnp.where(low, two, one), jnp.where(low, one, two)], axis=0)
        )
    from_north, from_south = swapped

    fields = [surface[...], transport[0], transport[1], levels[...], push_east[...], push_north[...]]
    height, east_bar, north_bar, force_east, force_north = subcycles(
        fields, packed[...], from_west, from_east, from_south, from_north, own_north, own_south, pad
    )
    shallow[0] = height
    shallow[1] = east_bar
    shallow[2] = north_bar
    flat = [
        pltpu.make_async_copy(shallow.at[0], height_out, sems.at[3]),
        pltpu.make_async_copy(shallow.at[pl.ds(1, 2)], transport_out, sems.at[4]),
    ]
    for copy in flat:
        copy.start()
    count = jnp.maximum(levels[...], 1.0)
    shallow[3] = east_bar - (sum_east[...] + depth * force_east) / count
    shallow[4] = north_bar - (sum_north[...] + depth * force_north) / count

    row = rows_of((8, nx))
    places = (0, ny - 8)
    parts = (row == 0, row == 7)
    signs = (1.0, -1.0)
    blocks = (from_south, from_north)
    slope = 0.5 * TIMESTEP * THERMAL_EXPANSION
    carried = [jnp.zeros((8, nx), jnp.float32) for _ in range(4)]
    wet = levels[...]
    step = depth // GROUPS
    slabs = []
    for k in range(depth):
        mask = wet > float(k)
        velocity[0, k] = jnp.where(mask, velocity_east[k] + shallow[3], 0.0)
        velocity[1, k, 8 : ny - 8] = jnp.where(
            mask[8 : ny - 8], velocity_north[k, 8 : ny - 8] + shallow[4, 8 : ny - 8], 0.0
        )
        for s in (0, 1):
            place = pl.ds(places[s], 8)
            carried[s] += jnp.where(parts[s], signs[s] * slope * blocks[s][p_row + k : p_row + k + 1], 0.0)
            velocity[1, k, place] = jnp.where(
                mask[places[s] : places[s] + 8], velocity_north[k, place] + carried[s] + shallow[4, place], 0.0
            )
        if (k + 1) % step == 0:
            part = pl.ds(k + 1 - step, step)
            copy = pltpu.make_async_copy(velocity.at[:, part], velocity_out.at[:, part], sems.at[5 + k // step])
            copy.start()
            slabs.append(copy)
    solved = [[], []]
    for k in range(depth):
        for s in (0, 1):
            place = pl.ds(places[s], 8)
            mask = parts[s] & (wet[places[s] : places[s] + 8] > float(k))
            flux = blocks[s][f_row + k : f_row + k + 1]
            source = jnp.where(mask, signs[s] * 0.5 * TRANSPORT_SPEED * flux, 0.0)
            carried[2 + s] = source * inverses[k, place] + lowers[k, place] * carried[2 + s]
            solved[s].append(carried[2 + s])
    for s in (0, 1):
        place = pl.ds(places[s], 8)
        later = jnp.zeros((8, nx), jnp.float32)
        for k in range(depth - 1, -1, -1):
            later = solved[s][k] - ratios[k, place] * later
            rims[k, pl.ds(8 * s, 8)] = mixed[k, place] + later
    edges = [
        pltpu.make_async_copy(rims.at[:, pl.ds(0, 8)], mixed_out.at[:, pl.ds(0, 8)], sems.at[1]),
        pltpu.make_async_copy(rims.at[:, pl.ds(8, 8)], mixed_out.at[:, pl.ds(ny - 8, 8)], sems.at[2]),
    ]
    for copy in edges:
        copy.start()
    for copy in [middle] + edges + flat + slabs:
        copy.wait()


def partner(block, zonal, parity):
    sx, sy, sa = (lax.axis_size(a) for a in AXES)
    count = sx * sa
    pairs = []
    for x in range(count):
        for y in range(sy):
            tx, ty = x, y
            if zonal:
                tx = (x + 1 if x % 2 == parity else x - 1) % count
            else:
                ty = y + 1 if y % 2 == parity else y - 1
            if 0 <= ty < sy:
                source = (x // sa * sy + y) * sa + x % sa
                pairs.append((source, (tx // sa * sy + ty) * sa + tx % sa))
    return lax.ppermute(block, AXES, pairs)


def estimate(flops, moved):
    return pl.CostEstimate(flops=flops, bytes_accessed=moved, transcendentals=0)


def per_device(thermal, current, mixing, surface, transport, flag, wet):
    depth, ny, nx = thermal.shape
    total_rows = ny * lax.axis_size("gy")
    pad = -(-depth // 8) * 8
    f32 = jnp.float32
    here = pl.BlockSpec(memory_space=pltpu.VMEM)
    far = pl.BlockSpec(memory_space=pltpu.HBM)
    params = pltpu.CompilerParams(vmem_limit_bytes=VMEM_BYTES)
    rows = 6 * W + 2 * pad + 8
    sd = jax.ShapeDtypeStruct
    cube = sd((depth, ny, nx), f32)
    pair = sd((2, depth, ny, nx), f32)
    cells = depth * ny * nx
    plane = sd((ny, nx), f32)
    edge = sd((ny - FOLD_ROWS + 8, nx), f32)
    outs = pl.pallas_call(
        functools.partial(edges_kernel, total_rows),
        out_shape=[edge, edge, sd((rows, nx), f32), sd((rows, nx), f32)] + [plane] * 6 + [sd((24, ny, nx), f32)],
        in_specs=[far] * 6,
        out_specs=[here] * 10 + [far],
        scratch_shapes=[
            pltpu.VMEM((depth, ny, nx), f32),
            pltpu.VMEM((2, depth, ny, nx), f32),
            pltpu.VMEM((3, ny, nx), f32),
            pltpu.VMEM((2, 2 * pad, nx), f32),
            pltpu.VMEM((2, ny, nx), f32),
            pltpu.VMEM((ny, nx), jnp.int32),
            pltpu.VMEM((ny, nx), jnp.int32),
            pltpu.SemaphoreType.DMA((5 + 3 * GROUPS,)),
        ],
        compiler_params=pltpu.CompilerParams(vmem_limit_bytes=EDGES_VMEM),
        cost_estimate=estimate(30 * cells, 12 * cells),
        name="edges",
    )(thermal, current, surface, transport, flag, wet)
    first, second, to_first, to_second, packed, levels, sum_east, sum_north, force_east, force_north, ground = outs
    zonal_first = partner(first, True, 0)
    zonal_second = partner(second, True, 1)
    velocity_east, velocity_north, mixed, ratios, inverses, lowers = pl.pallas_call(
        functools.partial(columns_kernel, total_rows),
        out_shape=[cube] * 6,
        in_specs=[far] * 4,
        out_specs=[here] * 6,
        scratch_shapes=[
            pltpu.VMEM((4, ny, nx), f32),
            pltpu.VMEM((ny, nx), f32),
            pltpu.VMEM((depth, ny, nx), f32),
            pltpu.VMEM((2, depth, ny, nx), f32),
            pltpu.VMEM((depth, ny, nx), f32),
            pltpu.SemaphoreType.DMA((1 + 3 * GROUPS,)),
        ],
        compiler_params=pltpu.CompilerParams(vmem_limit_bytes=COLUMNS_VMEM),
        cost_estimate=estimate(100 * cells, 40 * cells),
        name="columns",
    )(thermal, current, mixing, ground)
    zonal_first, zonal_second, velocity_east = lax.optimization_barrier((zonal_first, zonal_second, velocity_east))
    even = lax.axis_index("gy") % 2 == 0
    tall = ny - FOLD_ROWS
    top = [zonal_first[tall - 8 :], zonal_second[tall - 8 :]]
    bottom = [zonal_first[:8], zonal_first[tall:], zonal_second[:8], zonal_second[tall:]]
    top = jnp.concatenate(top, axis=0)
    bottom = jnp.concatenate(bottom, axis=0)
    merid_first = partner(jnp.concatenate([to_first, jnp.where(even, top, bottom)], axis=0), False, 0)
    merid_second = partner(jnp.concatenate([to_second, jnp.where(even, bottom, top)], axis=0), False, 1)
    velocity_east, mixed = pl.pallas_call(
        zonal_kernel,
        out_shape=[cube, cube],
        in_specs=[here] * 8,
        out_specs=[here] * 2,
        scratch_shapes=[pltpu.VMEM((2, ny, nx), f32)],
        compiler_params=params,
        cost_estimate=estimate(20 * cells, 20 * cells),
        name="zonal",
    )(levels, zonal_first, zonal_second, velocity_east, mixed, ratios, inverses, lowers)
    return pl.pallas_call(
        finish_kernel,
        out_shape=[cube, pair, sd((ny, nx), f32), sd((2, ny, nx), f32)],
        in_specs=[here] * 20,
        out_specs=[far] * 4,
        scratch_shapes=[
            pltpu.VMEM((2, depth, ny, nx), f32),
            pltpu.VMEM((depth, 16, nx), f32),
            pltpu.VMEM((5, ny, nx), f32),
            pltpu.SemaphoreType.DMA((5 + GROUPS,)),
        ],
        compiler_params=params,
        name="finish",
    )(
        levels,
        surface,
        transport,
        sum_east,
        sum_north,
        force_east,
        force_north,
        packed,
        to_first,
        to_second,
        zonal_first,
        zonal_second,
        merid_second,
        merid_first,
        velocity_east,
        velocity_north,
        mixed,
        ratios,
        inverses,
        lowers,
    )


def solution(mesh):
    placed = (
        P(None, "gy", ("gx", "ga")),
        P(None, None, "gy", ("gx", "ga")),
        P(None, "gy", ("gx", "ga")),
        P("gy", ("gx", "ga")),
        P(None, "gy", ("gx", "ga")),
        P("gy", ("gx", "ga")),
        P("gy", ("gx", "ga")),
    )
    return jax.shard_map(
        per_device,
        mesh=mesh,
        in_specs=placed,
        out_specs=(
            P(None, "gy", ("gx", "ga")),
            P(None, None, "gy", ("gx", "ga")),
            P("gy", ("gx", "ga")),
            P(None, "gy", ("gx", "ga")),
        ),
        check_vma=False,
    )
```

```python
import functools

import jax
import jax.numpy as jnp
from jax import lax
from jax.experimental import pallas as pl
from jax.experimental.pallas import tpu as pltpu
from jax.sharding import PartitionSpec as P

NSUB = 4
W = 8
TRANSPORT_SPEED = 0.2
MIXING = 1.0
THERMAL_EXPANSION = 0.05
TIMESTEP = 0.2
SUBSTEP = 0.3
GRAVITY = 1.0

AXES = ("gx", "gy", "ga")
FIELDS = 6
FLUX_LANE = 20
FIELD_LANE = 40
WIDTHS = (7, 7, 6, 6, 5, 4)
FREE_LANE = 75
EDGE_ROWS = 80
WIDE = 53
PIECES = tuple(((1 + i, FREE_LANE), (t, p)) for i, (t, p) in enumerate(((7, 75), (7, 97), (8, 75), (8, 97), (0, 99), (9, 99))))
GROUPS = 4
CHUNK = 16
SLABS = (4, 6, 6, 4)
UNROLL = 5
BACK_UNROLL = 4
VMEM_BYTES = 24 * 1024 * 1024
EDGES_VMEM = 54608 * 1024
COLUMNS_VMEM = 46 * 1024 * 1024


def lanes_of(shape):
    return lax.broadcasted_iota(jnp.int32, shape, len(shape) - 1)


def rows_of(shape):
    return lax.broadcasted_iota(jnp.int32, shape, len(shape) - 2)


def roll_lanes(x, amount):
    amount = amount % x.shape[-1] if isinstance(amount, int) else amount
    return x if isinstance(amount, int) and amount == 0 else pltpu.roll(x, amount, x.ndim - 1)


def roll_rows(x, amount):
    return pltpu.roll(x, amount % x.shape[-2], x.ndim - 2)


def coriolis_of(shape, row_start, total_rows):
    rows = (rows_of(shape) + row_start).astype(jnp.float32)
    return 0.3 + 0.4 * rows / total_rows


def fold(full, edges):
    ny, nx = full.shape
    lane = lanes_of((8, nx))
    half = EDGE_ROWS // 2
    tiles = [full[8 * i : 8 * i + 8] for i in range(half // 8)]
    tiles += [full[ny - half + 8 * i : ny - half + 8 * i + 8] for i in range(half // 8)]
    pad = edges[0].shape[0]
    for tile, block, shift_by in ((0, edges[0], edges[2]), (len(tiles) - 1, edges[1], edges[2])):
        for group in range(pad // 8):
            place = FREE_LANE + 8 * group
            mine = (lane >= place) & (lane < place + 8)
            tiles[tile] = jnp.where(mine, roll_lanes(block[8 * group : 8 * group + 8], place - shift_by), tiles[tile])
    for i, ((wide, place), (narrow, spot)) in enumerate(PIECES):
        middle = full[half + 8 * i : half + 8 * i + 8]
        tiles[wide] = jnp.where(lane >= place, roll_lanes(middle, place), tiles[wide])
        mine = (lane >= spot) & (lane < spot + FREE_LANE - WIDE)
        tiles[narrow] = jnp.where(mine, roll_lanes(middle, spot - WIDE), tiles[narrow])
    return jnp.concatenate(tiles, axis=0)


def unfold(folded):
    nx = folded.shape[1]
    lane = lanes_of((8, nx))
    tiles = []
    for (wide, place), (narrow, spot) in PIECES:
        one = roll_lanes(folded[8 * wide : 8 * wide + 8], -place)
        two = roll_lanes(folded[8 * narrow : 8 * narrow + 8], WIDE - spot)
        tiles.append(jnp.where(lane < WIDE, one, two))
    half = EDGE_ROWS // 2
    return jnp.concatenate([folded[:half], *tiles, folded[half:]], axis=0)


def edges_kernel(
    total_rows,
    thermal,
    current,
    surface,
    transport,
    flag,
    wet,
    first,
    second,
    to_first,
    to_second,
    packed,
    levels_here,
    sum_east,
    sum_north,
    force_east,
    force_north,
    ground,
    thermal_here,
    current_here,
    bars_here,
    edge_rows,
    packs,
    flag_here,
    wet_here,
    sems,
):
    depth, ny, nx = thermal.shape
    shape = (ny, nx)
    pad = -(-depth // 8) * 8
    masks = [
        pltpu.make_async_copy(flag, flag_here, sems.at[0]),
        pltpu.make_async_copy(wet, wet_here, sems.at[1]),
    ]
    slabs = []
    begin = 0
    for g, count in enumerate(SLABS):
        part = pl.ds(begin, count)
        begin += count
        slabs.append(
            [
                pltpu.make_async_copy(thermal.at[part], thermal_here.at[part], sems.at[3 + 3 * g]),
                pltpu.make_async_copy(current.at[0, part], current_here.at[0, part], sems.at[4 + 3 * g]),
                pltpu.make_async_copy(current.at[1, part], current_here.at[1, part], sems.at[5 + 3 * g]),
            ]
        )
    bars = [
        pltpu.make_async_copy(surface, bars_here.at[0], sems.at[3 + 3 * GROUPS]),
        pltpu.make_async_copy(transport, bars_here.at[pl.ds(1, 2)], sems.at[4 + 3 * GROUPS]),
    ]
    for copy in masks + [c for slab in slabs for c in slab] + bars:
        copy.start()
    lane = lanes_of(shape)
    zero = jnp.zeros(shape, jnp.float32)
    packs[0] = zero
    packs[1] = zero
    for ref in (sum_east, sum_north, force_east, force_north):
        ref[...] = zero
    edge_rows[...] = jnp.zeros(edge_rows.shape, jnp.float32)
    for copy in masks:
        copy.wait()
    levels_here[...] = (flag_here[...] * wet_here[...]).astype(jnp.float32)
    floor = pltpu.make_async_copy(levels_here, ground.at[0], sems.at[2])
    floor.start()

    def chunk(begin, count, start):
        inner = pl.ds(start, CHUNK)
        low, high = max(start - 8, 0), min(start + CHUNK + 8, ny)
        deep = levels_here[low:high]
        mine = slice(start - low, start - low + CHUNK)
        part = lanes_of((CHUNK, nx))
        row = rows_of((CHUNK, nx))
        totals = [ref[inner] for ref in (sum_east, sum_north, force_east, force_north)]
        east, west = packs[0, inner], packs[1, inner]
        for k in range(begin, begin + count):
            weight = jnp.maximum(deep[mine] - float(k), 0.0)
            mask = weight > 0.0
            wide = jnp.where(deep > float(k), thermal_here[k, low:high], 0.0)
            t = wide[mine]
            u = current_here[0, k, inner]
            v = current_here[1, k, inner]
            totals[0] += jnp.where(mask, u, 0.0)
            totals[1] += jnp.where(mask, v, 0.0)
            ahead = jnp.where(part == nx - 1, 0.0, roll_lanes(t, nx - 1))
            behind = jnp.where(part == 0, 0.0, roll_lanes(t, 1))
            totals[2] += weight * (ahead - behind)
            above = roll_rows(wide, -1)[mine]
            below = roll_rows(wide, 1)[mine]
            if high == ny:
                above = jnp.where(row == CHUNK - 1, 0.0, above)
            if low == 0:
                below = jnp.where(row == 0, 0.0, below)
            totals[3] += weight * (above - below)
            moved = roll_lanes(t, k + 1)
            flux = roll_lanes(u * t, FLUX_LANE + k + 1)
            east = jnp.where(part == k, moved, jnp.where(part == FLUX_LANE + k, flux, east))
            west = jnp.where(part == k + 1, moved, jnp.where(part == FLUX_LANE + k + 1, flux, west))
            if start == 0:
                edge_rows[0, k : k + 1, :] = t[:1]
                edge_rows[0, pad + k : pad + k + 1, :] = v[:1] * t[:1]
            if start == ny - CHUNK:
                edge_rows[1, k : k + 1, :] = t[CHUNK - 1 :]
                edge_rows[1, pad + k : pad + k + 1, :] = v[CHUNK - 1 :] * t[CHUNK - 1 :]
        for ref, total in zip((sum_east, sum_north, force_east, force_north), totals):
            ref[inner] = total
        packs[0, inner], packs[1, inner] = east, west

    begin = 0
    for slab, count in zip(slabs, SLABS):
        for copy in slab:
            copy.wait()
        for start in range(0, ny, CHUNK):
            chunk(begin, count, start)
        begin += count
    for copy in bars:
        copy.wait()
    levels = levels_here[...]
    east = packs[0]
    west = roll_lanes(packs[1], nx - 1)
    own = jnp.where(lane < FLUX_LANE, east, roll_lanes(west, FLUX_LANE))
    packed[...] = own
    scale = TIMESTEP / depth
    slope = 0.5 * THERMAL_EXPANSION
    f = coriolis_of(shape, lax.axis_index("gy") * ny, total_rows)
    push_east = scale * (f * sum_north[...] - slope * force_east[...])
    push_north = scale * (-f * sum_east[...] - slope * force_north[...])
    force_east[...] = push_east
    force_north[...] = push_north
    low = lax.axis_index("ga") == 0
    even = lax.axis_index("gy") % 2 == 0
    for i, field in enumerate([bars_here[0], bars_here[1], bars_here[2], levels, push_east, push_north]):
        to_first[W * i : W * (i + 1), :] = jnp.where(even, field[ny - W :], field[:W])
        to_second[W * i : W * (i + 1), :] = jnp.where(even, field[:W], field[ny - W :])
    height = bars_here[0]
    east_bar = bars_here[1] + SUBSTEP * push_east
    north_bar = bars_here[2] + SUBSTEP * push_north
    pull = (0.5 * SUBSTEP * GRAVITY / depth) * levels
    east_next = jnp.where(levels > 0.0, east_bar, 0.0) - pull * (roll_lanes(height, nx - 1) - roll_lanes(height, 1))
    last = WIDTHS[1] - 1
    east_bar = jnp.where((lane == last) | (lane == nx - 1 - last), east_next, east_bar)
    place = FIELD_LANE
    for field, width in zip([height, east_bar, north_bar, levels, push_east, push_north], WIDTHS):
        mine = (lane >= place) & (lane < place + width)
        west = jnp.where(mine, roll_lanes(field, place), west)
        east = jnp.where(mine, roll_lanes(field, place - (nx - width)), east)
        place += width
    rims = [edge_rows[0, :pad], edge_rows[1, :pad]]
    east = fold(east, [*rims, nx - W])
    west = fold(west, [*rims, 0])
    first[...] = jnp.where(low, east, west)
    second[...] = jnp.where(low, west, east)
    start = 6 * W
    base = start + 2 * pad
    to_first[start:base, :] = jnp.where(even, edge_rows[1], edge_rows[0])
    to_second[start:base, :] = jnp.where(even, edge_rows[0], edge_rows[1])
    to_first[base:, :] = jnp.where(even, own[ny - 8 :], own[:8])
    to_second[base:, :] = jnp.where(even, own[:8], own[ny - 8 :])
    floor.wait()


def edge_matrices(nx):
    row = rows_of((nx, nx))
    lane = lanes_of((nx, nx))
    first = lane < FLUX_LANE
    second = (lane >= FLUX_LANE) & (lane < 2 * FLUX_LANE)
    copy = jnp.where((first & (row == 0)) | (second & (row == nx - 1)), 1.0, 0.0)
    first = (row < FLUX_LANE) & (lane == 0)
    second = (row >= FLUX_LANE) & (row < 2 * FLUX_LANE) & (lane == nx - 1)
    return copy, jnp.where(first, 1.0, jnp.where(second, -1.0, 0.0))


def across_edges(values, levels, copy, add):
    lane = lanes_of(values.shape)
    levels = jnp.dot(levels, copy, preferred_element_type=jnp.float32)
    weight = jnp.maximum(levels - jnp.where(lane < FLUX_LANE, lane, lane - FLUX_LANE).astype(jnp.float32), 0.0)
    terms = jnp.where(lane < 2 * FLUX_LANE, weight * values, 0.0)
    return jnp.dot(terms, add, precision=lax.Precision.HIGHEST, preferred_element_type=jnp.float32)


def row_sum(values, levels):
    weight = jnp.maximum(levels - rows_of(values.shape).astype(jnp.float32), 0.0)
    return jnp.sum(weight * values, axis=0, keepdims=True)


def unfold_rows(east_block, west_block, pad):
    nx = east_block.shape[1]
    lane = lanes_of(east_block.shape)
    out = []
    for group in range(pad // 8):
        place = FREE_LANE + 8 * group
        out.append(
            jnp.where(
                lane < W,
                roll_lanes(east_block, -place),
                jnp.where(lane >= nx - W, roll_lanes(west_block, nx - W - place), 0.0),
            )
        )
    return jnp.concatenate(out, axis=0)


def subcycles(tank, fields, packed, from_west, from_east, from_south, from_north, own_north, own_south, pad):
    ny, nx = packed.shape
    p_row = 6 * W
    base = p_row + 2 * pad + 8
    west = jnp.concatenate([from_south[base : base + 8], unfold(from_west), from_north[base : base + 8]], axis=0)
    east = jnp.concatenate([from_south[base + 8 : base + 16], unfold(from_east), from_north[base + 8 : base + 16]], axis=0)
    mine = jnp.concatenate([from_south[base - 8 : base], packed, from_north[base - 8 : base]], axis=0)
    lane = lanes_of(west.shape)
    row = rows_of(west.shape)
    centres = []
    halos = []
    place = FIELD_LANE
    for i, (field, width) in enumerate(zip(fields, WIDTHS)):
        centres.append(jnp.concatenate([from_south[W * i : W * (i + 1)], field, from_north[W * i : W * (i + 1)]], axis=0))
        halos.append(
            jnp.where(
                lane < width,
                roll_lanes(east, -place),
                jnp.where(lane >= nx - width, roll_lanes(west, nx - width - place), 0.0),
            )
        )
        place += width
    depth_centre, depth_halo = centres[3], halos[3]
    share = TIMESTEP / 20.0 * 0.5 * THERMAL_EXPANSION
    copy, add = edge_matrices(nx)
    beyond = jnp.where(lane < FLUX_LANE, west, roll_lanes(east, FLUX_LANE))
    centres[4] = centres[4] + share * across_edges(beyond, depth_centre, copy, add)
    lacking = share * across_edges(mine, depth_halo, copy, add)
    halos[4] = halos[4] + lacking
    halos[1] = halos[1] + SUBSTEP * lacking
    north_beyond = (
        from_north[p_row : p_row + pad],
        unfold_rows(from_north[base + 8 : base + 16], from_north[base : base + 8], pad),
    )
    south_beyond = (
        from_south[p_row : p_row + pad],
        unfold_rows(from_south[base + 8 : base + 16], from_south[base : base + 8], pad),
    )
    end = EDGE_ROWS - 8
    north_edge = (own_north, unfold_rows(from_east[end:], from_west[end:], pad))
    south_edge = (own_south, unfold_rows(from_east[:8], from_west[:8], pad))
    for part, fields, depths in ((0, centres, depth_centre), (1, halos, depth_halo)):
        top, bottom = W + ny - 1, W
        lacking = (
            jnp.where(row == bottom, share * row_sum(south_beyond[part], depths[bottom : bottom + 1]), 0.0)
            - jnp.where(row == top, share * row_sum(north_beyond[part], depths[top : top + 1]), 0.0)
            + jnp.where(row == top + 1, share * row_sum(north_edge[part], depths[top + 1 : top + 2]), 0.0)
            - jnp.where(row == bottom - 1, share * row_sum(south_edge[part], depths[bottom - 1 : bottom]), 0.0)
        )
        fields[5] = fields[5] + lacking
        if part:
            fields[2] = fields[2] + SUBSTEP * lacking
    centres[1] = centres[1] + SUBSTEP * centres[4]
    centres[2] = centres[2] + SUBSTEP * centres[5]
    inner = slice(W, W + ny)
    forces = centres[4][inner], centres[5][inner]
    lines = ny + 2 * W
    last = WIDTHS[1] - 1
    given = (lane == last) | (lane == nx - 1 - last)
    zero = jnp.zeros((8, 2 * nx), jnp.float32)
    for i in (0, 2):
        tank[i, :8, :] = zero
        tank[i, lines + 8 :, :] = zero
    for half, (height, east_bar, north_bar, water, force_east, force_north) in enumerate((centres, halos)):
        place = slice(half * nx, (half + 1) * nx)
        wet = water > 0.0
        pull = (0.5 * SUBSTEP * GRAVITY / 20.0) * water
        tank[0, 8 : lines + 8, place] = height
        tank[1, 8 : lines + 8, place] = jnp.where(wet | given if half else wet, east_bar, 0.0)
        tank[2, 8 : lines + 8, place] = jnp.where(wet, north_bar, 0.0)
        tank[3, 8 : lines + 8, place] = pull
        tank[4, 8 : lines + 8, place] = jnp.where(wet, SUBSTEP * force_east, 0.0)
        tank[5, 8 : lines + 8, place] = jnp.where(wet, SUBSTEP * force_north, 0.0)
        tank[6, 8 : lines + 8, place] = jnp.where(wet, 0.5 * SUBSTEP, 0.0)
        tank[7, 8 : lines + 8, place] = jnp.where(given, 0.0, pull) if half else pull

    def across(x):
        return roll_lanes(x, 2 * nx - 1) - roll_lanes(x, 1)

    for step in range(NSUB):
        final = step == NSUB - 1
        for start in range(8, lines + 8, 8):
            here, above, below = (pl.ds(start + i, 8) for i in (0, 1, -1))
            whole = not final or 8 < start < lines
            if whole:
                east_bar = tank[1, here] - tank[3 if step else 7, here] * across(tank[0, here])
                tank[1, here] = east_bar + tank[4, here] if step else east_bar
            north_bar = tank[2, here] - tank[3, here] * (tank[0, above] - tank[0, below])
            tank[2, here] = north_bar + tank[5, here] if step else north_bar
        for start in range(16 if final else 8, lines if final else lines + 8, 8):
            here, above, below = (pl.ds(start + i, 8) for i in (0, 1, -1))
            if final:
                turn = across(tank[1, here])[:, :nx] + (tank[2, above, :nx] - tank[2, below, :nx])
                tank[0, here, :nx] = tank[0, here, :nx] - tank[6, here, :nx] * turn
            else:
                turn = across(tank[1, here]) + (tank[2, above] - tank[2, below])
                tank[0, here] = tank[0, here] - tank[6, here] * turn
    mine = pl.ds(8 + W, ny)
    return tank[0, mine, :nx], tank[1, mine, :nx], tank[2, mine, :nx], *forces


def ahead_less_behind(x):
    lane = lanes_of(x.shape)
    nx = x.shape[1]
    return jnp.where(lane == nx - 1, 0.0, roll_lanes(x, nx - 1)) - jnp.where(lane == 0, 0.0, roll_lanes(x, 1))


def above_less_below(x):
    row = rows_of(x.shape)
    ny = x.shape[0]
    return jnp.where(row == ny - 1, 0.0, roll_rows(x, ny - 1)) - jnp.where(row == 0, 0.0, roll_rows(x, 1))


def columns_kernel(
    total_rows,
    thermal,
    current,
    mixing,
    ground,
    velocity_east,
    velocity_north,
    mixed,
    ratios,
    inverses,
    lowers,
    planes,
    levels,
    thermal_here,
    current_here,
    mixing_here,
    sems,
):
    depth, ny, nx = thermal.shape
    shape = (ny, nx)
    step = depth // GROUPS
    floor = pltpu.make_async_copy(ground.at[0], levels, sems.at[0])
    floor.start()
    slabs = []
    for g in range(GROUPS):
        part = pl.ds(g * step, step)
        more = pl.ds(g * step, step + 1) if g == 0 else pl.ds(g * step + 1, min(step, depth - g * step - 1))
        slabs.append(
            [
                pltpu.make_async_copy(thermal.at[part], thermal_here.at[part], sems.at[1 + 3 * g]),
                pltpu.make_async_copy(current.at[:, part], current_here.at[:, part], sems.at[2 + 3 * g]),
                pltpu.make_async_copy(mixing.at[more], mixing_here.at[more], sems.at[3 + 3 * g]),
            ]
        )
        for copy in slabs[-1]:
            copy.start()
    zero = jnp.zeros(shape, jnp.float32)
    planes[0] = zero
    planes[1] = zero
    planes[2] = zero
    planes[3] = TIMESTEP * coriolis_of(shape, lax.axis_index("gy") * ny, total_rows)
    ratios[0] = zero
    mixed[0] = zero
    slope = 0.5 * TIMESTEP * THERMAL_EXPANSION
    floor.wait()

    def forward(k, carry):
        wet = levels[...]
        mask = wet > lax.convert_element_type(k, jnp.float32)
        raw = thermal_here[k]
        t = jnp.where(mask, raw, 0.0)
        u = current_here[0, k]
        v = current_here[1, k]
        dx = planes[0] + slope * ahead_less_behind(t)
        dy = planes[1] + slope * above_less_below(t)
        planes[0] = dx
        planes[1] = dy
        turn = planes[3]
        velocity_east[k] = u + turn * v - dx
        velocity_north[k] = v - turn * u - dy
        spread = ahead_less_behind(u * t) + above_less_below(v * t)
        source = jnp.where(mask, raw - 0.5 * TRANSPORT_SPEED * spread, 0.0)
        below = jnp.minimum(k + 1, depth - 1)
        upper = jnp.where(
            wet > lax.convert_element_type(k + 1, jnp.float32), 0.5 * MIXING * (mixing_here[k] + mixing_here[below]), 0.0
        )
        lower = planes[2]
        planes[2] = upper
        above = jnp.maximum(k - 1, 0)
        inverse = 1.0 / (1.0 + upper + lower * (1.0 + ratios[above]))
        lower = lower * inverse
        inverses[k] = inverse
        lowers[k] = lower
        ratios[k] = -upper * inverse
        mixed[k] = source * inverse + lower * mixed[above]
        return carry

    for g in range(GROUPS):
        for copy in slabs[g]:
            copy.wait()
        lax.fori_loop(g * step, (g + 1) * step, forward, 0, unroll=UNROLL)

    def backward(i, carry):
        k = depth - 2 - i
        mixed[k] = mixed[k] - ratios[k] * mixed[k + 1]
        return carry

    lax.fori_loop(0, depth - 1, backward, 0, unroll=BACK_UNROLL)


def zonal_kernel(levels, from_first, from_second, velocity, mixed, ratios, inverses, lowers, velocity_out, mixed_out, planes):
    depth, ny, nx = mixed.shape
    shape = (ny, nx)
    lane = lanes_of(shape)
    low = lax.axis_index("ga") == 0
    from_east = unfold(jnp.where(low, from_first[...], from_second[...]))
    from_west = unfold(jnp.where(low, from_second[...], from_first[...]))
    spot = rows_of((nx, nx))
    place = lanes_of((nx, nx))
    spread_east = jnp.where((place == 2 * spot) & (spot < FIELD_LANE), 1.0, 0.0)
    spread_west = jnp.where((place == 2 * spot + 1) & (spot < FIELD_LANE), 1.0, 0.0)

    def spread(x, where):
        return jnp.dot(x, where, precision=lax.Precision.HIGHEST, preferred_element_type=jnp.float32)

    halo = spread(from_west, spread_west) - spread(from_east, spread_east)
    slope = 0.5 * TIMESTEP * THERMAL_EXPANSION
    planes[0] = jnp.where(lane < 2 * FLUX_LANE, slope, 0.5 * TRANSPORT_SPEED) * halo
    zero = jnp.zeros(shape, jnp.float32)
    planes[1] = zero
    mixed_out[0] = zero

    def forward(k, carry):
        edge = (lane == 0) | (lane == nx - 1)
        mask = edge & (levels[...] > lax.convert_element_type(k, jnp.float32))
        push = planes[1] + jnp.where(edge, roll_lanes(planes[0], nx - 1 - 2 * k), 0.0)
        planes[1] = push
        velocity_out[k] = velocity[k] + push
        source = jnp.where(mask, roll_lanes(planes[0], nx - 1 - 2 * FLUX_LANE - 2 * k), 0.0)
        above = jnp.maximum(k - 1, 0)
        mixed_out[k] = source * inverses[k] + lowers[k] * mixed_out[above]
        return carry

    lax.fori_loop(0, depth, forward, 0, unroll=UNROLL)

    def backward(i, later):
        k = depth - 1 - i
        now = mixed_out[k] - ratios[k] * planes[1]
        planes[1] = now
        mixed_out[k] = mixed[k] + now
        return later

    planes[1] = zero
    lax.fori_loop(0, depth, backward, 0, unroll=BACK_UNROLL)


def finish_kernel(
    levels,
    surface,
    transport,
    sum_east,
    sum_north,
    push_east,
    push_north,
    packed,
    own_first,
    own_second,
    zonal_first,
    zonal_second,
    merid_second,
    merid_first,
    velocity_east,
    velocity_north,
    mixed,
    ratios,
    inverses,
    lowers,
    mixed_out,
    velocity_out,
    height_out,
    transport_out,
    velocity,
    rims,
    shallow,
    tank,
    sems,
):
    depth, ny, nx = mixed.shape
    pad = -(-depth // 8) * 8
    p_row, f_row = 6 * W, 6 * W + pad
    middle = pltpu.make_async_copy(mixed.at[:, pl.ds(8, ny - 16)], mixed_out.at[:, pl.ds(8, ny - 16)], sems.at[0])
    middle.start()
    low = lax.axis_index("ga") == 0
    even = lax.axis_index("gy") % 2 == 0

    def choose(test, a, b):
        return jnp.where(test, a[...], b[...]), jnp.where(test, b[...], a[...])

    from_east, from_west = choose(low, zonal_first, zonal_second)
    from_north, from_south = choose(even, merid_first, merid_second)
    own_north, own_south = choose(even, own_first.at[pl.ds(p_row, pad)], own_second.at[pl.ds(p_row, pad)])
    base = f_row + pad + 8
    swapped = []
    for block in (from_north, from_south):
        one, two = block[base : base + 8], block[base + 8 : base + 16]
        swapped.append(
            jnp.concatenate([block[:base], jnp.where(low, two, one), jnp.where(low, one, two)], axis=0)
        )
    from_north, from_south = swapped

    fields = [surface[...], transport[0], transport[1], levels[...], push_east[...], push_north[...]]
    height, east_bar, north_bar, force_east, force_north = subcycles(
        tank, fields, packed[...], from_west, from_east, from_south, from_north, own_north, own_south, pad
    )
    shallow[0] = height
    shallow[1] = east_bar
    shallow[2] = north_bar
    flat = [
        pltpu.make_async_copy(shallow.at[0], height_out, sems.at[3]),
        pltpu.make_async_copy(shallow.at[pl.ds(1, 2)], transport_out, sems.at[4]),
    ]
    for copy in flat:
        copy.start()
    count = jnp.maximum(levels[...], 1.0)
    shallow[3] = east_bar - (sum_east[...] + depth * force_east) / count
    shallow[4] = north_bar - (sum_north[...] + depth * force_north) / count

    row = rows_of((8, nx))
    places = (0, ny - 8)
    parts = (row == 0, row == 7)
    signs = (1.0, -1.0)
    blocks = (from_south, from_north)
    slope = 0.5 * TIMESTEP * THERMAL_EXPANSION
    carried = [jnp.zeros((8, nx), jnp.float32) for _ in range(4)]
    wet = levels[...]
    step = depth // GROUPS
    slabs = []
    for k in range(depth):
        mask = wet > float(k)
        velocity[0, k] = jnp.where(mask, velocity_east[k] + shallow[3], 0.0)
        velocity[1, k, 8 : ny - 8] = jnp.where(
            mask[8 : ny - 8], velocity_north[k, 8 : ny - 8] + shallow[4, 8 : ny - 8], 0.0
        )
        for s in (0, 1):
            place = pl.ds(places[s], 8)
            carried[s] += jnp.where(parts[s], signs[s] * slope * blocks[s][p_row + k : p_row + k + 1], 0.0)
            velocity[1, k, place] = jnp.where(
                mask[places[s] : places[s] + 8], velocity_north[k, place] + carried[s] + shallow[4, place], 0.0
            )
        if (k + 1) % step == 0:
            part = pl.ds(k + 1 - step, step)
            copy = pltpu.make_async_copy(velocity.at[:, part], velocity_out.at[:, part], sems.at[5 + k // step])
            copy.start()
            slabs.append(copy)
    solved = [[], []]
    for k in range(depth):
        for s in (0, 1):
            place = pl.ds(places[s], 8)
            mask = parts[s] & (wet[places[s] : places[s] + 8] > float(k))
            flux = blocks[s][f_row + k : f_row + k + 1]
            source = jnp.where(mask, signs[s] * 0.5 * TRANSPORT_SPEED * flux, 0.0)
            carried[2 + s] = source * inverses[k, place] + lowers[k, place] * carried[2 + s]
            solved[s].append(carried[2 + s])
    for s in (0, 1):
        place = pl.ds(places[s], 8)
        later = jnp.zeros((8, nx), jnp.float32)
        for k in range(depth - 1, -1, -1):
            later = solved[s][k] - ratios[k, place] * later
            rims[k, pl.ds(8 * s, 8)] = mixed[k, place] + later
    edges = [
        pltpu.make_async_copy(rims.at[:, pl.ds(0, 8)], mixed_out.at[:, pl.ds(0, 8)], sems.at[1]),
        pltpu.make_async_copy(rims.at[:, pl.ds(8, 8)], mixed_out.at[:, pl.ds(ny - 8, 8)], sems.at[2]),
    ]
    for copy in edges:
        copy.start()
    for copy in [middle] + edges + flat + slabs:
        copy.wait()


def partner(block, zonal, parity):
    sx, sy, sa = (lax.axis_size(a) for a in AXES)
    count = sx * sa
    pairs = []
    for x in range(count):
        for y in range(sy):
            tx, ty = x, y
            if zonal:
                tx = (x + 1 if x % 2 == parity else x - 1) % count
            else:
                ty = y + 1 if y % 2 == parity else y - 1
            if 0 <= ty < sy:
                source = (x // sa * sy + y) * sa + x % sa
                pairs.append((source, (tx // sa * sy + ty) * sa + tx % sa))
    return lax.ppermute(block, AXES, pairs)


def estimate(flops, moved):
    return pl.CostEstimate(flops=flops, bytes_accessed=moved, transcendentals=0)


def per_device(thermal, current, mixing, surface, transport, flag, wet):
    depth, ny, nx = thermal.shape
    total_rows = ny * lax.axis_size("gy")
    pad = -(-depth // 8) * 8
    f32 = jnp.float32
    here = pl.BlockSpec(memory_space=pltpu.VMEM)
    far = pl.BlockSpec(memory_space=pltpu.HBM)
    params = pltpu.CompilerParams(vmem_limit_bytes=VMEM_BYTES)
    rows = 6 * W + 2 * pad + 8
    sd = jax.ShapeDtypeStruct
    cube = sd((depth, ny, nx), f32)
    pair = sd((2, depth, ny, nx), f32)
    cells = depth * ny * nx
    plane = sd((ny, nx), f32)
    edge = sd((EDGE_ROWS, nx), f32)
    outs = pl.pallas_call(
        functools.partial(edges_kernel, total_rows),
        out_shape=[edge, edge, sd((rows, nx), f32), sd((rows, nx), f32)] + [plane] * 6 + [sd((24, ny, nx), f32)],
        in_specs=[far] * 6,
        out_specs=[here] * 10 + [far],
        scratch_shapes=[
            pltpu.VMEM((depth, ny, nx), f32),
            pltpu.VMEM((2, depth, ny, nx), f32),
            pltpu.VMEM((3, ny, nx), f32),
            pltpu.VMEM((2, 2 * pad, nx), f32),
            pltpu.VMEM((2, ny, nx), f32),
            pltpu.VMEM((ny, nx), jnp.int32),
            pltpu.VMEM((ny, nx), jnp.int32),
            pltpu.SemaphoreType.DMA((5 + 3 * GROUPS,)),
        ],
        compiler_params=pltpu.CompilerParams(vmem_limit_bytes=EDGES_VMEM),
        cost_estimate=estimate(30 * cells, 12 * cells),
        name="edges",
    )(thermal, current, surface, transport, flag, wet)
    first, second, to_first, to_second, packed, levels, sum_east, sum_north, force_east, force_north, ground = outs
    zonal_first = partner(first, True, 0)
    zonal_second = partner(second, True, 1)
    velocity_east, velocity_north, mixed, ratios, inverses, lowers = pl.pallas_call(
        functools.partial(columns_kernel, total_rows),
        out_shape=[cube] * 6,
        in_specs=[far] * 4,
        out_specs=[here] * 6,
        scratch_shapes=[
            pltpu.VMEM((4, ny, nx), f32),
            pltpu.VMEM((ny, nx), f32),
            pltpu.VMEM((depth, ny, nx), f32),
            pltpu.VMEM((2, depth, ny, nx), f32),
            pltpu.VMEM((depth, ny, nx), f32),
            pltpu.SemaphoreType.DMA((1 + 3 * GROUPS,)),
        ],
        compiler_params=pltpu.CompilerParams(vmem_limit_bytes=COLUMNS_VMEM),
        cost_estimate=estimate(100 * cells, 40 * cells),
        name="columns",
    )(thermal, current, mixing, ground)
    zonal_first, zonal_second, velocity_east = lax.optimization_barrier((zonal_first, zonal_second, velocity_east))
    even = lax.axis_index("gy") % 2 == 0
    end = EDGE_ROWS - 8
    top = jnp.concatenate([zonal_first[end:], zonal_second[end:]], axis=0)
    bottom = jnp.concatenate([zonal_first[:8], zonal_second[:8]], axis=0)
    merid_first = partner(jnp.concatenate([to_first, jnp.where(even, top, bottom)], axis=0), False, 0)
    merid_second = partner(jnp.concatenate([to_second, jnp.where(even, bottom, top)], axis=0), False, 1)
    velocity_east, mixed = pl.pallas_call(
        zonal_kernel,
        out_shape=[cube, cube],
        in_specs=[here] * 8,
        out_specs=[here] * 2,
        scratch_shapes=[pltpu.VMEM((2, ny, nx), f32)],
        compiler_params=params,
        cost_estimate=estimate(20 * cells, 20 * cells),
        name="zonal",
    )(levels, zonal_first, zonal_second, velocity_east, mixed, ratios, inverses, lowers)
    return pl.pallas_call(
        finish_kernel,
        out_shape=[cube, pair, sd((ny, nx), f32), sd((2, ny, nx), f32)],
        in_specs=[here] * 20,
        out_specs=[far] * 4,
        scratch_shapes=[
            pltpu.VMEM((2, depth, ny, nx), f32),
            pltpu.VMEM((depth, 16, nx), f32),
            pltpu.VMEM((5, ny, nx), f32),
            pltpu.VMEM((8, ny + 4 * W, 2 * nx), f32),
            pltpu.SemaphoreType.DMA((5 + GROUPS,)),
        ],
        compiler_params=params,
        name="finish",
    )(
        levels,
        surface,
        transport,
        sum_east,
        sum_north,
        force_east,
        force_north,
        packed,
        to_first,
        to_second,
        zonal_first,
        zonal_second,
        merid_second,
        merid_first,
        velocity_east,
        velocity_north,
        mixed,
        ratios,
        inverses,
        lowers,
    )


def solution(mesh):
    placed = (
        P(None, "gy", ("gx", "ga")),
        P(None, None, "gy", ("gx", "ga")),
        P(None, "gy", ("gx", "ga")),
        P("gy", ("gx", "ga")),
        P(None, "gy", ("gx", "ga")),
        P("gy", ("gx", "ga")),
        P("gy", ("gx", "ga")),
    )
    return jax.shard_map(
        per_device,
        mesh=mesh,
        in_specs=placed,
        out_specs=(
            P(None, "gy", ("gx", "ga")),
            P(None, None, "gy", ("gx", "ga")),
            P("gy", ("gx", "ga")),
            P(None, "gy", ("gx", "ga")),
        ),
        check_vma=False,
    )
```

```python
import functools

import jax
import jax.numpy as jnp
from jax import lax
from jax.experimental import pallas as pl
from jax.experimental.pallas import tpu as pltpu
from jax.sharding import PartitionSpec as P

NSUB = 4
W = 8
TRANSPORT_SPEED = 0.2
MIXING = 1.0
THERMAL_EXPANSION = 0.05
TIMESTEP = 0.2
SUBSTEP = 0.3
GRAVITY = 1.0

AXES = ("gx", "gy", "ga")
FIELDS = 6
FLUX_LANE = 20
FIELD_LANE = 40
WIDTHS = (7, 7, 6, 6, 5, 4)
FREE_LANE = 75
EDGE_ROWS = 80
WIDE = 53
PIECES = tuple(((1 + i, FREE_LANE), (t, p)) for i, (t, p) in enumerate(((7, 75), (7, 97), (8, 75), (8, 97), (0, 99), (9, 99))))
GROUPS = 4
CHUNK = 16
SLABS = (4, 6, 6, 4)
UNROLL = 5
BACK_UNROLL = 4
VMEM_BYTES = 24 * 1024 * 1024
EDGES_VMEM = 54608 * 1024
COLUMNS_VMEM = 46 * 1024 * 1024


def lanes_of(shape):
    return lax.broadcasted_iota(jnp.int32, shape, len(shape) - 1)


def rows_of(shape):
    return lax.broadcasted_iota(jnp.int32, shape, len(shape) - 2)


def roll_lanes(x, amount):
    amount = amount % x.shape[-1] if isinstance(amount, int) else amount
    return x if isinstance(amount, int) and amount == 0 else pltpu.roll(x, amount, x.ndim - 1)


def roll_rows(x, amount):
    return pltpu.roll(x, amount % x.shape[-2], x.ndim - 2)


def coriolis_of(shape, row_start, total_rows):
    rows = (rows_of(shape) + row_start).astype(jnp.float32)
    return 0.3 + 0.4 * rows / total_rows


def fold(full, edges):
    ny, nx = full.shape
    lane = lanes_of((8, nx))
    half = EDGE_ROWS // 2
    tiles = [full[8 * i : 8 * i + 8] for i in range(half // 8)]
    tiles += [full[ny - half + 8 * i : ny - half + 8 * i + 8] for i in range(half // 8)]
    pad = edges[0].shape[0]
    for tile, block, shift_by in ((0, edges[0], edges[2]), (len(tiles) - 1, edges[1], edges[2])):
        for group in range(pad // 8):
            place = FREE_LANE + 8 * group
            mine = (lane >= place) & (lane < place + 8)
            tiles[tile] = jnp.where(mine, roll_lanes(block[8 * group : 8 * group + 8], place - shift_by), tiles[tile])
    for i, ((wide, place), (narrow, spot)) in enumerate(PIECES):
        middle = full[half + 8 * i : half + 8 * i + 8]
        tiles[wide] = jnp.where(lane >= place, roll_lanes(middle, place), tiles[wide])
        mine = (lane >= spot) & (lane < spot + FREE_LANE - WIDE)
        tiles[narrow] = jnp.where(mine, roll_lanes(middle, spot - WIDE), tiles[narrow])
    return jnp.concatenate(tiles, axis=0)


def unfold(folded):
    nx = folded.shape[1]
    lane = lanes_of((8, nx))
    tiles = []
    for (wide, place), (narrow, spot) in PIECES:
        one = roll_lanes(folded[8 * wide : 8 * wide + 8], -place)
        two = roll_lanes(folded[8 * narrow : 8 * narrow + 8], WIDE - spot)
        tiles.append(jnp.where(lane < WIDE, one, two))
    half = EDGE_ROWS // 2
    return jnp.concatenate([folded[:half], *tiles, folded[half:]], axis=0)


def edges_kernel(
    total_rows,
    thermal,
    current,
    surface,
    transport,
    flag,
    wet,
    first,
    second,
    to_first,
    to_second,
    packed,
    levels_here,
    sum_east,
    sum_north,
    force_east,
    force_north,
    ground,
    thermal_here,
    current_here,
    bars_here,
    edge_rows,
    packs,
    flag_here,
    wet_here,
    sems,
):
    depth, ny, nx = thermal.shape
    shape = (ny, nx)
    pad = -(-depth // 8) * 8
    masks = [
        pltpu.make_async_copy(flag, flag_here, sems.at[0]),
        pltpu.make_async_copy(wet, wet_here, sems.at[1]),
    ]
    slabs = []
    begin = 0
    for g, count in enumerate(SLABS):
        part = pl.ds(begin, count)
        begin += count
        slabs.append(
            [
                pltpu.make_async_copy(thermal.at[part], thermal_here.at[part], sems.at[3 + 3 * g]),
                pltpu.make_async_copy(current.at[0, part], current_here.at[0, part], sems.at[4 + 3 * g]),
                pltpu.make_async_copy(current.at[1, part], current_here.at[1, part], sems.at[5 + 3 * g]),
            ]
        )
    bars = [
        pltpu.make_async_copy(surface, bars_here.at[0], sems.at[3 + 3 * GROUPS]),
        pltpu.make_async_copy(transport, bars_here.at[pl.ds(1, 2)], sems.at[4 + 3 * GROUPS]),
    ]
    for copy in masks + [c for slab in slabs for c in slab] + bars:
        copy.start()
    lane = lanes_of(shape)
    zero = jnp.zeros(shape, jnp.float32)
    packs[0] = zero
    packs[1] = zero
    for ref in (sum_east, sum_north, force_east, force_north):
        ref[...] = zero
    edge_rows[...] = jnp.zeros(edge_rows.shape, jnp.float32)
    for copy in masks:
        copy.wait()
    levels_here[...] = (flag_here[...] * wet_here[...]).astype(jnp.float32)
    floor = pltpu.make_async_copy(levels_here, ground.at[0], sems.at[2])
    floor.start()

    def chunk(begin, count, start):
        inner = pl.ds(start, CHUNK)
        low, high = max(start - 8, 0), min(start + CHUNK + 8, ny)
        deep = levels_here[low:high]
        mine = slice(start - low, start - low + CHUNK)
        part = lanes_of((CHUNK, nx))
        row = rows_of((CHUNK, nx))
        totals = [ref[inner] for ref in (sum_east, sum_north, force_east, force_north)]
        east, west = packs[0, inner], packs[1, inner]
        for k in range(begin, begin + count):
            weight = jnp.maximum(deep[mine] - float(k), 0.0)
            mask = weight > 0.0
            wide = jnp.where(deep > float(k), thermal_here[k, low:high], 0.0)
            t = wide[mine]
            u = current_here[0, k, inner]
            v = current_here[1, k, inner]
            totals[0] += jnp.where(mask, u, 0.0)
            totals[1] += jnp.where(mask, v, 0.0)
            ahead = jnp.where(part == nx - 1, 0.0, roll_lanes(t, nx - 1))
            behind = jnp.where(part == 0, 0.0, roll_lanes(t, 1))
            totals[2] += weight * (ahead - behind)
            above = roll_rows(wide, -1)[mine]
            below = roll_rows(wide, 1)[mine]
            if high == ny:
                above = jnp.where(row == CHUNK - 1, 0.0, above)
            if low == 0:
                below = jnp.where(row == 0, 0.0, below)
            totals[3] += weight * (above - below)
            moved = roll_lanes(t, k + 1)
            flux = roll_lanes(u * t, FLUX_LANE + k + 1)
            east = jnp.where(part == k, moved, jnp.where(part == FLUX_LANE + k, flux, east))
            west = jnp.where(part == k + 1, moved, jnp.where(part == FLUX_LANE + k + 1, flux, west))
            if start == 0:
                edge_rows[0, k : k + 1, :] = t[:1]
                edge_rows[0, pad + k : pad + k + 1, :] = v[:1] * t[:1]
            if start == ny - CHUNK:
                edge_rows[1, k : k + 1, :] = t[CHUNK - 1 :]
                edge_rows[1, pad + k : pad + k + 1, :] = v[CHUNK - 1 :] * t[CHUNK - 1 :]
        for ref, total in zip((sum_east, sum_north, force_east, force_north), totals):
            ref[inner] = total
        packs[0, inner], packs[1, inner] = east, west

    begin = 0
    for slab, count in zip(slabs, SLABS):
        for copy in slab:
            copy.wait()
        for start in range(0, ny, CHUNK):
            chunk(begin, count, start)
        begin += count
    for copy in bars:
        copy.wait()
    levels = levels_here[...]
    east = packs[0]
    west = roll_lanes(packs[1], nx - 1)
    own = jnp.where(lane < FLUX_LANE, east, roll_lanes(west, FLUX_LANE))
    packed[...] = own
    scale = TIMESTEP / depth
    slope = 0.5 * THERMAL_EXPANSION
    f = coriolis_of(shape, lax.axis_index("gy") * ny, total_rows)
    push_east = scale * (f * sum_north[...] - slope * force_east[...])
    push_north = scale * (-f * sum_east[...] - slope * force_north[...])
    force_east[...] = push_east
    force_north[...] = push_north
    low = lax.axis_index("ga") == 0
    even = lax.axis_index("gy") % 2 == 0
    for i, field in enumerate([bars_here[0], bars_here[1], bars_here[2], levels, push_east, push_north]):
        to_first[W * i : W * (i + 1), :] = jnp.where(even, field[ny - W :], field[:W])
        to_second[W * i : W * (i + 1), :] = jnp.where(even, field[:W], field[ny - W :])
    height = bars_here[0]
    east_bar = bars_here[1] + SUBSTEP * push_east
    north_bar = bars_here[2] + SUBSTEP * push_north
    pull = (0.5 * SUBSTEP * GRAVITY / depth) * levels
    east_next = jnp.where(levels > 0.0, east_bar, 0.0) - pull * (roll_lanes(height, nx - 1) - roll_lanes(height, 1))
    last = WIDTHS[1] - 1
    east_bar = jnp.where((lane == last) | (lane == nx - 1 - last), east_next, east_bar)
    place = FIELD_LANE
    for field, width in zip([height, east_bar, north_bar, levels, push_east, push_north], WIDTHS):
        mine = (lane >= place) & (lane < place + width)
        west = jnp.where(mine, roll_lanes(field, place), west)
        east = jnp.where(mine, roll_lanes(field, place - (nx - width)), east)
        place += width
    rims = [edge_rows[0, :pad], edge_rows[1, :pad]]
    east = fold(east, [*rims, nx - W])
    west = fold(west, [*rims, 0])
    first[...] = jnp.where(low, east, west)
    second[...] = jnp.where(low, west, east)
    start = 6 * W
    base = start + 2 * pad
    to_first[start:base, :] = jnp.where(even, edge_rows[1], edge_rows[0])
    to_second[start:base, :] = jnp.where(even, edge_rows[0], edge_rows[1])
    to_first[base:, :] = jnp.where(even, own[ny - 8 :], own[:8])
    to_second[base:, :] = jnp.where(even, own[:8], own[ny - 8 :])
    floor.wait()


def edge_matrices(nx):
    row = rows_of((nx, nx))
    lane = lanes_of((nx, nx))
    first = lane < FLUX_LANE
    second = (lane >= FLUX_LANE) & (lane < 2 * FLUX_LANE)
    copy = jnp.where((first & (row == 0)) | (second & (row == nx - 1)), 1.0, 0.0)
    first = (row < FLUX_LANE) & (lane == 0)
    second = (row >= FLUX_LANE) & (row < 2 * FLUX_LANE) & (lane == nx - 1)
    return copy, jnp.where(first, 1.0, jnp.where(second, -1.0, 0.0))


def across_edges(values, levels, copy, add):
    lane = lanes_of(values.shape)
    levels = jnp.dot(levels, copy, preferred_element_type=jnp.float32)
    weight = jnp.maximum(levels - jnp.where(lane < FLUX_LANE, lane, lane - FLUX_LANE).astype(jnp.float32), 0.0)
    terms = jnp.where(lane < 2 * FLUX_LANE, weight * values, 0.0)
    return jnp.dot(terms, add, precision=lax.Precision.HIGHEST, preferred_element_type=jnp.float32)


def row_sum(values, levels):
    weight = jnp.maximum(levels - rows_of(values.shape).astype(jnp.float32), 0.0)
    return jnp.sum(weight * values, axis=0, keepdims=True)


def unfold_rows(east_block, west_block, pad):
    nx = east_block.shape[1]
    lane = lanes_of(east_block.shape)
    out = []
    for group in range(pad // 8):
        place = FREE_LANE + 8 * group
        out.append(
            jnp.where(
                lane < W,
                roll_lanes(east_block, -place),
                jnp.where(lane >= nx - W, roll_lanes(west_block, nx - W - place), 0.0),
            )
        )
    return jnp.concatenate(out, axis=0)


def subcycles(tank, fields, packed, from_west, from_east, from_south, from_north, own_north, own_south, pad):
    ny, nx = packed.shape
    p_row = 6 * W
    base = p_row + 2 * pad + 8
    west = jnp.concatenate([from_south[base : base + 8], unfold(from_west), from_north[base : base + 8]], axis=0)
    east = jnp.concatenate([from_south[base + 8 : base + 16], unfold(from_east), from_north[base + 8 : base + 16]], axis=0)
    mine = jnp.concatenate([from_south[base - 8 : base], packed, from_north[base - 8 : base]], axis=0)
    lane = lanes_of(west.shape)
    row = rows_of(west.shape)
    centres = []
    halos = []
    place = FIELD_LANE
    for i, (field, width) in enumerate(zip(fields, WIDTHS)):
        centres.append(jnp.concatenate([from_south[W * i : W * (i + 1)], field, from_north[W * i : W * (i + 1)]], axis=0))
        halos.append(
            jnp.where(
                lane < width,
                roll_lanes(east, -place),
                jnp.where(lane >= nx - width, roll_lanes(west, nx - width - place), 0.0),
            )
        )
        place += width
    depth_centre, depth_halo = centres[3], halos[3]
    share = TIMESTEP / 20.0 * 0.5 * THERMAL_EXPANSION
    copy, add = edge_matrices(nx)
    beyond = jnp.where(lane < FLUX_LANE, west, roll_lanes(east, FLUX_LANE))
    centres[4] = centres[4] + share * across_edges(beyond, depth_centre, copy, add)
    lacking = share * across_edges(mine, depth_halo, copy, add)
    halos[4] = halos[4] + lacking
    halos[1] = halos[1] + SUBSTEP * lacking
    north_beyond = (
        from_north[p_row : p_row + pad],
        unfold_rows(from_north[base + 8 : base + 16], from_north[base : base + 8], pad),
    )
    south_beyond = (
        from_south[p_row : p_row + pad],
        unfold_rows(from_south[base + 8 : base + 16], from_south[base : base + 8], pad),
    )
    end = EDGE_ROWS - 8
    north_edge = (own_north, unfold_rows(from_east[end:], from_west[end:], pad))
    south_edge = (own_south, unfold_rows(from_east[:8], from_west[:8], pad))
    for part, fields, depths in ((0, centres, depth_centre), (1, halos, depth_halo)):
        top, bottom = W + ny - 1, W
        lacking = (
            jnp.where(row == bottom, share * row_sum(south_beyond[part], depths[bottom : bottom + 1]), 0.0)
            - jnp.where(row == top, share * row_sum(north_beyond[part], depths[top : top + 1]), 0.0)
            + jnp.where(row == top + 1, share * row_sum(north_edge[part], depths[top + 1 : top + 2]), 0.0)
            - jnp.where(row == bottom - 1, share * row_sum(south_edge[part], depths[bottom - 1 : bottom]), 0.0)
        )
        fields[5] = fields[5] + lacking
        if part:
            fields[2] = fields[2] + SUBSTEP * lacking
    centres[1] = centres[1] + SUBSTEP * centres[4]
    centres[2] = centres[2] + SUBSTEP * centres[5]
    inner = slice(W, W + ny)
    forces = centres[4][inner], centres[5][inner]
    lines = ny + 2 * W
    last = WIDTHS[1] - 1
    given = (lane == last) | (lane == nx - 1 - last)
    zero = jnp.zeros((8, 2 * nx), jnp.float32)
    for i in (0, 2):
        tank[i, :8, :] = zero
        tank[i, lines + 8 :, :] = zero
    for half, (height, east_bar, north_bar, water, force_east, force_north) in enumerate((centres, halos)):
        place = slice(half * nx, (half + 1) * nx)
        wet = water > 0.0
        pull = (0.5 * SUBSTEP * GRAVITY / 20.0) * water
        tank[0, 8 : lines + 8, place] = height
        tank[1, 8 : lines + 8, place] = jnp.where(wet | given if half else wet, east_bar, 0.0)
        tank[2, 8 : lines + 8, place] = jnp.where(wet, north_bar, 0.0)
        tank[3, 8 : lines + 8, place] = pull
        tank[4, 8 : lines + 8, place] = jnp.where(wet, SUBSTEP * force_east, 0.0)
        tank[5, 8 : lines + 8, place] = jnp.where(wet, SUBSTEP * force_north, 0.0)
        tank[6, 8 : lines + 8, place] = jnp.where(wet, 0.5 * SUBSTEP, 0.0)
        tank[7, 8 : lines + 8, place] = jnp.where(given, 0.0, pull) if half else pull

    def across(x):
        return roll_lanes(x, 2 * nx - 1) - roll_lanes(x, 1)

    for step in range(NSUB):
        final = step == NSUB - 1
        for start in range(8, lines + 8, 8):
            here, above, below = (pl.ds(start + i, 8) for i in (0, 1, -1))
            whole = not final or 8 < start < lines
            if whole:
                east_bar = tank[1, here] - tank[3 if step else 7, here] * across(tank[0, here])
                tank[1, here] = east_bar + tank[4, here] if step else east_bar
            north_bar = tank[2, here] - tank[3, here] * (tank[0, above] - tank[0, below])
            tank[2, here] = north_bar + tank[5, here] if step else north_bar
        for start in range(16 if final else 8, lines if final else lines + 8, 8):
            here, above, below = (pl.ds(start + i, 8) for i in (0, 1, -1))
            if final:
                turn = across(tank[1, here])[:, :nx] + (tank[2, above, :nx] - tank[2, below, :nx])
                tank[0, here, :nx] = tank[0, here, :nx] - tank[6, here, :nx] * turn
            else:
                turn = across(tank[1, here]) + (tank[2, above] - tank[2, below])
                tank[0, here] = tank[0, here] - tank[6, here] * turn
    mine = pl.ds(8 + W, ny)
    return tank[0, mine, :nx], tank[1, mine, :nx], tank[2, mine, :nx], *forces


def ahead_less_behind(x):
    lane = lanes_of(x.shape)
    nx = x.shape[1]
    return jnp.where(lane == nx - 1, 0.0, roll_lanes(x, nx - 1)) - jnp.where(lane == 0, 0.0, roll_lanes(x, 1))


def above_less_below(x):
    row = rows_of(x.shape)
    ny = x.shape[0]
    return jnp.where(row == ny - 1, 0.0, roll_rows(x, ny - 1)) - jnp.where(row == 0, 0.0, roll_rows(x, 1))


def columns_kernel(
    total_rows,
    thermal,
    current,
    mixing,
    ground,
    velocity_east,
    velocity_north,
    mixed,
    ratios,
    inverses,
    lowers,
    planes,
    levels,
    thermal_here,
    current_here,
    mixing_here,
    sems,
):
    depth, ny, nx = thermal.shape
    shape = (ny, nx)
    step = depth // GROUPS
    floor = pltpu.make_async_copy(ground.at[0], levels, sems.at[0])
    floor.start()
    slabs = []
    for g in range(GROUPS):
        part = pl.ds(g * step, step)
        more = pl.ds(g * step, step + 1) if g == 0 else pl.ds(g * step + 1, min(step, depth - g * step - 1))
        slabs.append(
            [
                pltpu.make_async_copy(thermal.at[part], thermal_here.at[part], sems.at[1 + 3 * g]),
                pltpu.make_async_copy(current.at[:, part], current_here.at[:, part], sems.at[2 + 3 * g]),
                pltpu.make_async_copy(mixing.at[more], mixing_here.at[more], sems.at[3 + 3 * g]),
            ]
        )
        for copy in slabs[-1]:
            copy.start()
    zero = jnp.zeros(shape, jnp.float32)
    planes[0] = zero
    planes[1] = zero
    planes[2] = zero
    planes[3] = TIMESTEP * coriolis_of(shape, lax.axis_index("gy") * ny, total_rows)
    ratios[0] = zero
    mixed[0] = zero
    slope = 0.5 * TIMESTEP * THERMAL_EXPANSION
    floor.wait()

    def forward(k, carry):
        wet = levels[...]
        mask = wet > lax.convert_element_type(k, jnp.float32)
        raw = thermal_here[k]
        t = jnp.where(mask, raw, 0.0)
        u = current_here[0, k]
        v = current_here[1, k]
        dx = planes[0] + slope * ahead_less_behind(t)
        dy = planes[1] + slope * above_less_below(t)
        planes[0] = dx
        planes[1] = dy
        turn = planes[3]
        velocity_east[k] = u + turn * v - dx
        velocity_north[k] = v - turn * u - dy
        spread = ahead_less_behind(u * t) + above_less_below(v * t)
        source = jnp.where(mask, raw - 0.5 * TRANSPORT_SPEED * spread, 0.0)
        below = jnp.minimum(k + 1, depth - 1)
        upper = jnp.where(
            wet > lax.convert_element_type(k + 1, jnp.float32), 0.5 * MIXING * (mixing_here[k] + mixing_here[below]), 0.0
        )
        lower = planes[2]
        planes[2] = upper
        above = jnp.maximum(k - 1, 0)
        inverse = 1.0 / (1.0 + upper + lower * (1.0 + ratios[above]))
        lower = lower * inverse
        inverses[k] = inverse
        lowers[k] = lower
        ratios[k] = -upper * inverse
        mixed[k] = source * inverse + lower * mixed[above]
        return carry

    for g in range(GROUPS):
        for copy in slabs[g]:
            copy.wait()
        lax.fori_loop(g * step, (g + 1) * step, forward, 0, unroll=UNROLL)

    def backward(i, carry):
        k = depth - 2 - i
        mixed[k] = mixed[k] - ratios[k] * mixed[k + 1]
        return carry

    lax.fori_loop(0, depth - 1, backward, 0, unroll=BACK_UNROLL)


def zonal_kernel(levels, from_first, from_second, velocity, mixed, ratios, inverses, lowers, velocity_out, mixed_out, planes):
    depth, ny, nx = mixed.shape
    shape = (ny, nx)
    lane = lanes_of(shape)
    low = lax.axis_index("ga") == 0
    from_east = unfold(jnp.where(low, from_first[...], from_second[...]))
    from_west = unfold(jnp.where(low, from_second[...], from_first[...]))
    spot = rows_of((nx, nx))
    place = lanes_of((nx, nx))
    spread_east = jnp.where((place == 2 * spot) & (spot < FIELD_LANE), 1.0, 0.0)
    spread_west = jnp.where((place == 2 * spot + 1) & (spot < FIELD_LANE), 1.0, 0.0)

    def spread(x, where):
        return jnp.dot(x, where, precision=lax.Precision.HIGHEST, preferred_element_type=jnp.float32)

    halo = spread(from_west, spread_west) - spread(from_east, spread_east)
    slope = 0.5 * TIMESTEP * THERMAL_EXPANSION
    planes[0] = jnp.where(lane < 2 * FLUX_LANE, slope, 0.5 * TRANSPORT_SPEED) * halo
    zero = jnp.zeros(shape, jnp.float32)
    planes[1] = zero
    mixed_out[0] = zero

    def forward(k, carry):
        edge = (lane == 0) | (lane == nx - 1)
        mask = edge & (levels[...] > lax.convert_element_type(k, jnp.float32))
        push = planes[1] + jnp.where(edge, roll_lanes(planes[0], nx - 1 - 2 * k), 0.0)
        planes[1] = push
        velocity_out[k] = velocity[k] + push
        source = jnp.where(mask, roll_lanes(planes[0], nx - 1 - 2 * FLUX_LANE - 2 * k), 0.0)
        above = jnp.maximum(k - 1, 0)
        mixed_out[k] = source * inverses[k] + lowers[k] * mixed_out[above]
        return carry

    lax.fori_loop(0, depth, forward, 0, unroll=UNROLL)

    def backward(i, later):
        k = depth - 1 - i
        now = mixed_out[k] - ratios[k] * planes[1]
        planes[1] = now
        mixed_out[k] = mixed[k] + now
        return later

    planes[1] = zero
    lax.fori_loop(0, depth, backward, 0, unroll=BACK_UNROLL)


def finish_kernel(
    levels,
    surface,
    transport,
    sum_east,
    sum_north,
    push_east,
    push_north,
    packed,
    own_first,
    own_second,
    zonal_first,
    zonal_second,
    merid_second,
    merid_first,
    velocity_east,
    velocity_north,
    mixed,
    ratios,
    inverses,
    lowers,
    mixed_out,
    velocity_out,
    height_out,
    transport_out,
    velocity,
    rims,
    shallow,
    tank,
    sems,
):
    depth, ny, nx = mixed.shape
    pad = -(-depth // 8) * 8
    p_row, f_row = 6 * W, 6 * W + pad
    middle = pltpu.make_async_copy(mixed.at[:, pl.ds(8, ny - 16)], mixed_out.at[:, pl.ds(8, ny - 16)], sems.at[0])
    middle.start()
    low = lax.axis_index("ga") == 0
    even = lax.axis_index("gy") % 2 == 0

    def choose(test, a, b):
        return jnp.where(test, a[...], b[...]), jnp.where(test, b[...], a[...])

    from_east, from_west = choose(low, zonal_first, zonal_second)
    from_north, from_south = choose(even, merid_first, merid_second)
    here = lax.axis_index("gy")
    from_north = jnp.where(here == lax.axis_size("gy") - 1, 0.0, from_north)
    from_south = jnp.where(here == 0, 0.0, from_south)
    own_north, own_south = choose(even, own_first.at[pl.ds(p_row, pad)], own_second.at[pl.ds(p_row, pad)])
    base = f_row + pad + 8
    swapped = []
    for block in (from_north, from_south):
        one, two = block[base : base + 8], block[base + 8 : base + 16]
        swapped.append(
            jnp.concatenate([block[:base], jnp.where(low, two, one), jnp.where(low, one, two)], axis=0)
        )
    from_north, from_south = swapped

    fields = [surface[...], transport[0], transport[1], levels[...], push_east[...], push_north[...]]
    height, east_bar, north_bar, force_east, force_north = subcycles(
        tank, fields, packed[...], from_west, from_east, from_south, from_north, own_north, own_south, pad
    )
    shallow[0] = height
    shallow[1] = east_bar
    shallow[2] = north_bar
    flat = [
        pltpu.make_async_copy(shallow.at[0], height_out, sems.at[3]),
        pltpu.make_async_copy(shallow.at[pl.ds(1, 2)], transport_out, sems.at[4]),
    ]
    for copy in flat:
        copy.start()
    count = jnp.maximum(levels[...], 1.0)
    shallow[3] = east_bar - (sum_east[...] + depth * force_east) / count
    shallow[4] = north_bar - (sum_north[...] + depth * force_north) / count

    row = rows_of((8, nx))
    places = (0, ny - 8)
    parts = (row == 0, row == 7)
    signs = (1.0, -1.0)
    blocks = (from_south, from_north)
    slope = 0.5 * TIMESTEP * THERMAL_EXPANSION
    carried = [jnp.zeros((8, nx), jnp.float32) for _ in range(4)]
    wet = levels[...]
    step = depth // GROUPS
    slabs = []
    for k in range(depth):
        mask = wet > float(k)
        velocity[0, k] = jnp.where(mask, velocity_east[k] + shallow[3], 0.0)
        velocity[1, k, 8 : ny - 8] = jnp.where(
            mask[8 : ny - 8], velocity_north[k, 8 : ny - 8] + shallow[4, 8 : ny - 8], 0.0
        )
        for s in (0, 1):
            place = pl.ds(places[s], 8)
            carried[s] += jnp.where(parts[s], signs[s] * slope * blocks[s][p_row + k : p_row + k + 1], 0.0)
            velocity[1, k, place] = jnp.where(
                mask[places[s] : places[s] + 8], velocity_north[k, place] + carried[s] + shallow[4, place], 0.0
            )
        if (k + 1) % step == 0:
            part = pl.ds(k + 1 - step, step)
            copy = pltpu.make_async_copy(velocity.at[:, part], velocity_out.at[:, part], sems.at[5 + k // step])
            copy.start()
            slabs.append(copy)
    solved = [[], []]
    for k in range(depth):
        for s in (0, 1):
            place = pl.ds(places[s], 8)
            mask = parts[s] & (wet[places[s] : places[s] + 8] > float(k))
            flux = blocks[s][f_row + k : f_row + k + 1]
            source = jnp.where(mask, signs[s] * 0.5 * TRANSPORT_SPEED * flux, 0.0)
            carried[2 + s] = source * inverses[k, place] + lowers[k, place] * carried[2 + s]
            solved[s].append(carried[2 + s])
    for s in (0, 1):
        place = pl.ds(places[s], 8)
        later = jnp.zeros((8, nx), jnp.float32)
        for k in range(depth - 1, -1, -1):
            later = solved[s][k] - ratios[k, place] * later
            rims[k, pl.ds(8 * s, 8)] = mixed[k, place] + later
    edges = [
        pltpu.make_async_copy(rims.at[:, pl.ds(0, 8)], mixed_out.at[:, pl.ds(0, 8)], sems.at[1]),
        pltpu.make_async_copy(rims.at[:, pl.ds(8, 8)], mixed_out.at[:, pl.ds(ny - 8, 8)], sems.at[2]),
    ]
    for copy in edges:
        copy.start()
    for copy in [middle] + edges + flat + slabs:
        copy.wait()


def partner(block, zonal, parity):
    sx, sy, sa = (lax.axis_size(a) for a in AXES)
    count = sx * sa
    pairs = []
    for x in range(count):
        for y in range(sy):
            tx, ty = x, y
            if zonal:
                tx = (x + 1 if x % 2 == parity else x - 1) % count
            else:
                ty = (y + 1 if y % 2 == parity else y - 1) % sy
            source = (x // sa * sy + y) * sa + x % sa
            pairs.append((source, (tx // sa * sy + ty) * sa + tx % sa))
    return lax.ppermute(block, AXES, pairs)


def estimate(flops, moved):
    return pl.CostEstimate(flops=flops, bytes_accessed=moved, transcendentals=0)


def per_device(thermal, current, mixing, surface, transport, flag, wet):
    depth, ny, nx = thermal.shape
    total_rows = ny * lax.axis_size("gy")
    pad = -(-depth // 8) * 8
    f32 = jnp.float32
    here = pl.BlockSpec(memory_space=pltpu.VMEM)
    far = pl.BlockSpec(memory_space=pltpu.HBM)
    params = pltpu.CompilerParams(vmem_limit_bytes=VMEM_BYTES)
    rows = 6 * W + 2 * pad + 8
    sd = jax.ShapeDtypeStruct
    cube = sd((depth, ny, nx), f32)
    pair = sd((2, depth, ny, nx), f32)
    cells = depth * ny * nx
    plane = sd((ny, nx), f32)
    edge = sd((EDGE_ROWS, nx), f32)
    outs = pl.pallas_call(
        functools.partial(edges_kernel, total_rows),
        out_shape=[edge, edge, sd((rows, nx), f32), sd((rows, nx), f32)] + [plane] * 6 + [sd((24, ny, nx), f32)],
        in_specs=[far] * 6,
        out_specs=[here] * 10 + [far],
        scratch_shapes=[
            pltpu.VMEM((depth, ny, nx), f32),
            pltpu.VMEM((2, depth, ny, nx), f32),
            pltpu.VMEM((3, ny, nx), f32),
            pltpu.VMEM((2, 2 * pad, nx), f32),
            pltpu.VMEM((2, ny, nx), f32),
            pltpu.VMEM((ny, nx), jnp.int32),
            pltpu.VMEM((ny, nx), jnp.int32),
            pltpu.SemaphoreType.DMA((5 + 3 * GROUPS,)),
        ],
        compiler_params=pltpu.CompilerParams(vmem_limit_bytes=EDGES_VMEM),
        cost_estimate=estimate(30 * cells, 12 * cells),
        name="edges",
    )(thermal, current, surface, transport, flag, wet)
    first, second, to_first, to_second, packed, levels, sum_east, sum_north, force_east, force_north, ground = outs
    zonal_first = partner(first, True, 0)
    zonal_second = partner(second, True, 1)
    velocity_east, velocity_north, mixed, ratios, inverses, lowers = pl.pallas_call(
        functools.partial(columns_kernel, total_rows),
        out_shape=[cube] * 6,
        in_specs=[far] * 4,
        out_specs=[here] * 6,
        scratch_shapes=[
            pltpu.VMEM((4, ny, nx), f32),
            pltpu.VMEM((ny, nx), f32),
            pltpu.VMEM((depth, ny, nx), f32),
            pltpu.VMEM((2, depth, ny, nx), f32),
            pltpu.VMEM((depth, ny, nx), f32),
            pltpu.SemaphoreType.DMA((1 + 3 * GROUPS,)),
        ],
        compiler_params=pltpu.CompilerParams(vmem_limit_bytes=COLUMNS_VMEM),
        cost_estimate=estimate(100 * cells, 40 * cells),
        name="columns",
    )(thermal, current, mixing, ground)
    zonal_first, zonal_second, velocity_east = lax.optimization_barrier((zonal_first, zonal_second, velocity_east))
    even = lax.axis_index("gy") % 2 == 0
    end = EDGE_ROWS - 8
    top = jnp.concatenate([zonal_first[end:], zonal_second[end:]], axis=0)
    bottom = jnp.concatenate([zonal_first[:8], zonal_second[:8]], axis=0)
    merid_first = partner(jnp.concatenate([to_first, jnp.where(even, top, bottom)], axis=0), False, 0)
    merid_second = partner(jnp.concatenate([to_second, jnp.where(even, bottom, top)], axis=0), False, 1)
    velocity_east, mixed = pl.pallas_call(
        zonal_kernel,
        out_shape=[cube, cube],
        in_specs=[here] * 8,
        out_specs=[here] * 2,
        scratch_shapes=[pltpu.VMEM((2, ny, nx), f32)],
        compiler_params=params,
        cost_estimate=estimate(20 * cells, 20 * cells),
        name="zonal",
    )(levels, zonal_first, zonal_second, velocity_east, mixed, ratios, inverses, lowers)
    return pl.pallas_call(
        finish_kernel,
        out_shape=[cube, pair, sd((ny, nx), f32), sd((2, ny, nx), f32)],
        in_specs=[here] * 20,
        out_specs=[far] * 4,
        scratch_shapes=[
            pltpu.VMEM((2, depth, ny, nx), f32),
            pltpu.VMEM((depth, 16, nx), f32),
            pltpu.VMEM((5, ny, nx), f32),
            pltpu.VMEM((8, ny + 4 * W, 2 * nx), f32),
            pltpu.SemaphoreType.DMA((5 + GROUPS,)),
        ],
        compiler_params=params,
        name="finish",
    )(
        levels,
        surface,
        transport,
        sum_east,
        sum_north,
        force_east,
        force_north,
        packed,
        to_first,
        to_second,
        zonal_first,
        zonal_second,
        merid_second,
        merid_first,
        velocity_east,
        velocity_north,
        mixed,
        ratios,
        inverses,
        lowers,
    )


def solution(mesh):
    placed = (
        P(None, "gy", ("gx", "ga")),
        P(None, None, "gy", ("gx", "ga")),
        P(None, "gy", ("gx", "ga")),
        P("gy", ("gx", "ga")),
        P(None, "gy", ("gx", "ga")),
        P("gy", ("gx", "ga")),
        P("gy", ("gx", "ga")),
    )
    return jax.shard_map(
        per_device,
        mesh=mesh,
        in_specs=placed,
        out_specs=(
            P(None, "gy", ("gx", "ga")),
            P(None, None, "gy", ("gx", "ga")),
            P("gy", ("gx", "ga")),
            P(None, "gy", ("gx", "ga")),
        ),
        check_vma=False,
    )
```
